256 devices in a mesh: segment: 2 (over core), chan: 128 (over y, x, z).
Axes of the slice: x: 4, y: 4, z: 8, core: 2. Of those that a mesh axis runs over, the one named last changes fastest.
Arguments:
- records: bfloat16 [4, 10240, 7680], P(None, 'chan')
- fan_limit: int32 [512], replicated, may hold values from 1 to 5120, as said below
- sources: int32 [256], replicated, may hold values from 0 to 10239, as said below
Outputs:
- correlations: bfloat16 [256, 1024, 512], P('segment', 'chan')
The draws below stay inside these ranges and needn't reach their ends.
Inputs may be any that keep to these rules, and one draw needn't show every extreme that they name: `sources`: 256 distinct channel indices; 0 and 10239 are among them. `fan_limit`: one limit for each band bin; the limits 1 and 5120 both occur.
All inputs are finite; a program needn't handle non-finite values.
Results may differ from the reference program's by a relative error of at most 0.0085.
Values may be sent and summed in bfloat16 or wider, within the bound.
A program may use at most 192 MiB of HBM per device.

```python
import math
import jax
import jax.numpy as jnp
from jax import lax

NCH = 10240
NT = 7680
NF = 512
FLO = 32
NVS = 256
STRIDE = 10
LAGS = 512
MB = 4


def draw_records(key, part):
    key = jax.random.fold_in(key, 11)
    noise_key, gain_key, envelope_key = jax.random.split(key, 3)
    gains = jnp.exp(jax.random.uniform(gain_key, (1, NCH, 1), jnp.float32, 0.0, math.log(10.0)))
    envelope = jnp.exp(jax.random.uniform(envelope_key, (MB, 1, NT), jnp.float32, 0.0, math.log(10.0)))
    noise = jax.random.normal(noise_key, (MB, NCH, NT), jnp.float32)
    return (0.3 * noise * gains * envelope).astype(jnp.bfloat16)


def draw_fan_limit(key, part):
    key = jax.random.fold_in(key, 12)
    limits = jax.random.randint(key, (NF,), 1, NCH // 2 + 1, jnp.int32)
    limits = limits.at[0].set(1)
    return limits.at[NF - 1].set(NCH // 2)


def draw_sources(key, part):
    key = jax.random.fold_in(key, 13)
    pick_key, order_key = jax.random.split(key)
    middle = jax.random.permutation(pick_key, NCH - 2)[:NVS - 2].astype(jnp.int32) + 1
    values = jnp.concatenate([jnp.array([0, NCH - 1], jnp.int32), middle])
    order = jax.random.permutation(order_key, NVS)
    return values[order]


def setup_inputs(seed: int = 0) -> dict:
    streams_of = jax.random.split(jax.random.key(seed), 4)
    records = draw_records(jax.random.fold_in(streams_of[3], 71), 0)
    fan_limit = draw_fan_limit(jax.random.fold_in(streams_of[3], 71), 0)
    sources = draw_sources(jax.random.fold_in(streams_of[3], 71), 0)
    return dict(records=records, fan_limit=fan_limit, sources=sources)


epsilon = 1e-06

def time_table(anchor, length):
    steps_t = anchor + jnp.arange(length, dtype=jnp.int32)
    freqs = FLO + jnp.arange(NF, dtype=jnp.int32)
    phase = steps_t[:, None] * freqs[None, :] % NT
    angle = phase.astype(jnp.float32) * (2.0 * math.pi / NT)
    return jnp.concatenate([jnp.cos(angle), -jnp.sin(angle)], axis=1).astype(jnp.bfloat16)

def lag_table():
    lagged = jnp.arange(LAGS, dtype=jnp.int32) - LAGS // 2
    freqs = FLO + jnp.arange(NF, dtype=jnp.int32)
    phase = freqs[:, None] * lagged[None, :] % NT
    angle = phase.astype(jnp.float32) * (2.0 * math.pi / NT)
    return jnp.concatenate([jnp.cos(angle), -jnp.sin(angle)], axis=0).astype(jnp.bfloat16)

def reference(records, fan_limit, sources):
    dft_table = time_table(0, NT)
    scale_time = 1.0 / math.sqrt(NT)

    def transform(record):
        spectra = jnp.dot(record, dft_table, preferred_element_type=jnp.float32) * scale_time
        real_part = spectra[:, :NF]
        imag_part = spectra[:, NF:]
        power = lax.optimization_barrier(jnp.mean(real_part * real_part + imag_part * imag_part, axis=1, keepdims=True))
        factor = lax.rsqrt(power + epsilon)
        return ((real_part * factor).astype(jnp.bfloat16), (imag_part * factor).astype(jnp.bfloat16))
    white_real, white_imag = lax.map(transform, records)
    field = white_real.astype(jnp.float32) + 1j * white_imag.astype(jnp.float32)
    wavenumber = jnp.arange(NCH, dtype=jnp.int32)
    signed = jnp.where(wavenumber < NCH // 2, wavenumber, wavenumber - NCH)
    keep = jnp.abs(signed)[:, None] <= fan_limit[None, :]
    spectrum = jnp.fft.fft(field, axis=1) * keep[None, :, :]
    back = jnp.fft.ifft(spectrum, axis=1)
    filt_real = jnp.real(back).astype(jnp.bfloat16).astype(jnp.float32)
    filt_imag = jnp.imag(back).astype(jnp.bfloat16).astype(jnp.float32)
    rec_real = filt_real[:, ::STRIDE, :]
    rec_imag = filt_imag[:, ::STRIDE, :]
    src_real = jnp.transpose(filt_real[:, sources, :], (1, 0, 2))
    src_imag = jnp.transpose(filt_imag[:, sources, :], (1, 0, 2))
    lagging = lag_table()
    scale_lag = 1.0 / math.sqrt(MB * NF)

    def correlate(pair):
        one_real, one_imag = pair
        cross_real = lax.optimization_barrier(jnp.sum(one_real[:, None, :] * rec_real + one_imag[:, None, :] * rec_imag, axis=0))
        cross_imag = lax.optimization_barrier(jnp.sum(one_real[:, None, :] * rec_imag - one_imag[:, None, :] * rec_real, axis=0))
        stacked = jnp.concatenate([cross_real, cross_imag], axis=1).astype(jnp.bfloat16)
        result = jnp.dot(stacked, lagging, preferred_element_type=jnp.float32) * scale_lag
        return result.astype(jnp.bfloat16)
    return lax.map(correlate, (src_real, src_imag))
```

```python
import functools
import math

import jax
import jax.numpy as jnp
import numpy as np
from jax import lax
from jax.experimental import pallas as pl
from jax.experimental.pallas import tpu as pltpu
from jax.sharding import PartitionSpec as P

NCH = 10240
NT = 7680
NF = 512
FLO = 32
NVS = 256
STRIDE = 10
LAGS = 512
MB = 4

epsilon = 1e-06

SEG = 2
NY, NX, NZ = 4, 4, 8
CHIPS = NY * NX * NZ
CH_DEV = NCH // CHIPS
F_DEV = NF // CHIPS
M_DEV = MB // SEG
SEQS = F_DEV * M_DEV
RECS = CH_DEV // STRIDE
HALF = NVS // SEG
LANES = 128
WIDE = SEQS * CH_DEV
KBLOCK = 1280
MESH = pl.DeviceIdType.MESH
BF = jnp.bfloat16
F32 = jnp.float32


def as_bf16(array):
    return np.asarray(array, np.float32).astype(jnp.bfloat16)


def split(array):
    high = as_bf16(array)
    low = as_bf16(np.asarray(array, np.float64) - high.astype(np.float64))
    return high, low


def time_table():
    freqs = FLO + np.arange(NF, dtype=np.int64)
    phase = freqs[:, None] * np.arange(NT, dtype=np.int64)[None, :] % NT
    angle = phase.astype(np.float32) * np.float32(2.0 * math.pi / NT)
    return as_bf16(np.concatenate([np.cos(angle), -np.sin(angle)], axis=0))


def lag_table():
    lagged = np.arange(LAGS, dtype=np.int64) - LAGS // 2
    freqs = FLO + np.arange(NF, dtype=np.int64)
    phase = freqs[:, None] * lagged[None, :] % NT
    angle = phase.astype(np.float32) * np.float32(2.0 * math.pi / NT)
    return as_bf16(np.concatenate([np.cos(angle), -np.sin(angle)], axis=0))


def roots(rows, cols, modulus):
    phase = np.arange(rows)[:, None] * np.arange(cols)[None, :] % modulus
    angle = phase * (2.0 * math.pi / modulus)
    return np.cos(angle), -np.sin(angle)


def filter_tables():
    dr, di = roots(CHIPS, CHIPS, CHIPS)
    er = np.zeros((LANES, LANES))
    ei = np.zeros((LANES, LANES))
    er[:CH_DEV, :CH_DEV], ei[:CH_DEV, :CH_DEV] = roots(CH_DEV, CH_DEV, CH_DEV)
    tr = np.zeros((CHIPS, LANES))
    ti = np.zeros((CHIPS, LANES))
    tr[:, :CH_DEV], ti[:, :CH_DEV] = roots(CHIPS, CH_DEV, NCH)
    outer = np.block([[dr, -di], [di, dr]])
    inner = np.block([[er, ei], [-ei, er]])
    inner_back = np.block([[er, -ei], [ei, er]])
    outer_back = np.block([[dr, di], [-di, dr]])
    tables = np.stack([t for m in (outer, inner, inner_back, outer_back) for t in split(m)])
    twist = np.stack([tr, ti]).astype(np.float32)
    pick = np.zeros((2, SEQS, LANES, LANES), np.float32)
    for part in range(2):
        for q in range(SEQS):
            for u in range(RECS):
                pick[part, q, STRIDE * u, (q * 2 + part) * RECS + u] = 1.0
    return tables, twist, as_bf16(pick.reshape(2, SEQS * LANES, LANES))


def mm(left, right):
    return jnp.dot(left, right, preferred_element_type=F32)


def mm_nt(left, right):
    return lax.dot_general(left, right, (((1,), (1,)), ((), ())), preferred_element_type=F32)


def halves(value):
    high = value.astype(BF)
    return high, (value - high.astype(F32)).astype(BF)


def transform_kernel(seg_ref, rec_ref, table_ref, out_ref, acc):
    step = pl.program_id(0)
    piece = rec_ref[...].reshape(M_DEV * CH_DEV, KBLOCK)
    part = mm_nt(table_ref[...], piece)

    @pl.when(step == 0)
    def _():
        acc[...] = part

    @pl.when(step > 0)
    def _():
        acc[...] += part

    @pl.when(step == NT // KBLOCK - 1)
    def _():
        spectra = acc[...] * (1.0 / math.sqrt(NT))
        power = jnp.sum(spectra * spectra, axis=0, keepdims=True) * (1.0 / NF)
        white = spectra * lax.rsqrt(power + epsilon)
        blocks = [white[CHIPS * g : CHIPS * (g + 1)] for g in range(2 * F_DEV)]
        out_ref[...] = jnp.concatenate(blocks, axis=1).astype(BF)


def transform(records, table):
    segment = lax.axis_index("segment").astype(jnp.int32).reshape(1)
    return pl.pallas_call(
        transform_kernel,
        out_shape=jax.ShapeDtypeStruct((CHIPS, 2 * WIDE), BF),
        grid_spec=pltpu.PrefetchScalarGridSpec(
            num_scalar_prefetch=1,
            grid=(NT // KBLOCK,),
            in_specs=[
                pl.BlockSpec((M_DEV, CH_DEV, KBLOCK), lambda k, seg: (seg[0], 0, k)),
                pl.BlockSpec((2 * NF, KBLOCK), lambda k, seg: (0, k)),
            ],
            out_specs=pl.BlockSpec((CHIPS, 2 * WIDE), lambda k, seg: (0, 0)),
            scratch_shapes=[pltpu.VMEM((2 * NF, M_DEV * CH_DEV), F32)],
        ),
        compiler_params=pltpu.CompilerParams(vmem_limit_bytes=40 << 20),
        cost_estimate=pl.CostEstimate(
            flops=2 * 2 * NF * NT * M_DEV * CH_DEV, bytes_accessed=18 << 20, transcendentals=0
        ),
        name="transform",
    )(segment, records, table)


def filter_kernel(col_ref, limit_ref, src_ref, x_ref, tables, twist, pick, s_ref, r_ref):
    column = col_ref[0]
    x = x_ref[...]
    tail = jnp.zeros((CHIPS, LANES), BF)
    xs = jnp.concatenate(
        [
            jnp.concatenate([x[:, :WIDE], tail], axis=1),
            jnp.concatenate([x[:, WIDE:], tail], axis=1),
        ],
        axis=0,
    )
    first = mm(tables[0], xs) + mm(tables[1], xs)
    tr, ti = twist[0], twist[1]
    turned = []
    for q in range(SEQS):
        yr = first[:CHIPS, CH_DEV * q : CH_DEV * q + LANES]
        yi = first[CHIPS:, CH_DEV * q : CH_DEV * q + LANES]
        turned.append(jnp.concatenate([yr * tr - yi * ti, yr * ti + yi * tr], axis=1))
    high, low = halves(jnp.concatenate(turned, axis=0))
    wave = mm(high, tables[2]) + mm(high, tables[3]) + mm(low, tables[2])
    shape = (CHIPS, 2 * LANES)
    lane = lax.broadcasted_iota(jnp.int32, shape, 1) % LANES
    index = lax.broadcasted_iota(jnp.int32, shape, 0) + CHIPS * lane
    signed = jnp.where(index < NCH // 2, index, index - NCH)
    reach = jnp.where(index < NCH, jnp.abs(signed), NCH)
    kept = []
    for q in range(SEQS):
        limit = limit_ref[(q // M_DEV) * CHIPS + column]
        kept.append(jnp.where(reach <= limit, wave[CHIPS * q : CHIPS * (q + 1)], 0.0))
    high, low = halves(jnp.concatenate(kept, axis=0))
    back = mm(high, tables[4]) + mm(high, tables[5]) + mm(low, tables[4])
    real, imag = [], []
    for q in range(SEQS):
        ur = back[CHIPS * q : CHIPS * (q + 1), :LANES]
        ui = back[CHIPS * q : CHIPS * (q + 1), LANES:]
        real.append(ur * tr + ui * ti)
        imag.append(ui * tr - ur * ti)
    high, low = halves(
        jnp.concatenate([jnp.concatenate(real, axis=1), jnp.concatenate(imag, axis=1)], axis=0)
    )
    field = mm(tables[6], high) + mm(tables[6], low) + mm(tables[7], high)
    field = (field * (1.0 / NCH)).astype(BF)
    r_ref[...] = mm(field[:CHIPS], pick[0]) + mm(field[CHIPS:], pick[1])
    source = src_ref[...]
    chip = ((source.astype(F32) + 0.5) * (1.0 / CH_DEV)).astype(jnp.int32)
    inside = source - CH_DEV * chip
    rows = lax.broadcasted_iota(jnp.int32, (LANES, NVS), 0)
    hot_inside = jnp.where(rows == inside, 1.0, 0.0).astype(BF)
    hot_chip = jnp.where(rows == chip, 1.0, 0.0)
    lines = []
    for q in range(SEQS):
        for part in range(2):
            block = field[CHIPS * part : CHIPS * (part + 1), LANES * q : LANES * (q + 1)]
            chosen = mm(block, hot_inside) * hot_chip
            lines.append(jnp.sum(chosen, axis=0, keepdims=True))
    found = jnp.concatenate(lines, axis=0).astype(BF)
    s_ref[0] = found[:, :HALF]
    s_ref[1] = found[:, HALF:]


def fan_filter(mixed, limits, sources):
    tables, twist, pick = filter_tables()
    column = lax.axis_index("chan").astype(jnp.int32).reshape(1)
    smem = pl.BlockSpec(memory_space=pltpu.SMEM)
    vmem = pl.BlockSpec(memory_space=pltpu.VMEM)
    return pl.pallas_call(
        filter_kernel,
        out_shape=(
            jax.ShapeDtypeStruct((SEG, 2 * SEQS, HALF), BF),
            jax.ShapeDtypeStruct((CHIPS, LANES), F32),
        ),
        in_specs=[smem, smem, vmem, vmem, vmem, vmem, vmem],
        out_specs=(vmem, vmem),
        compiler_params=pltpu.CompilerParams(vmem_limit_bytes=40 << 20),
        cost_estimate=pl.CostEstimate(flops=4 << 30, bytes_accessed=4 << 20, transcendentals=0),
        name="fan_filter",
    )(
        column,
        limits,
        sources.reshape(1, NVS),
        mixed,
        jnp.asarray(tables),
        jnp.asarray(twist),
        jnp.asarray(pick),
    )


def spread_kernel(s_in, r_in, s_all, r_fin, rz, rx, sz_s, sz_r, sx_s, sx_r, sy_s, sy_r, rz_s, rz_r,
                  rx_s, rx_r, ry_s, ry_r, here):
    seg = lax.axis_index("segment")
    chan = lax.axis_index("chan")
    z = lax.rem(chan, NZ)
    plane = lax.div(chan, NZ)
    x = lax.rem(plane, NX)
    y = lax.div(plane, NX)

    def target(ds, dy, dx, dz):
        ty, tx, tz = lax.rem(y + dy, NY), lax.rem(x + dx, NX), lax.rem(z + dz, NZ)
        return (lax.rem(seg + ds, SEG), (ty * NX + tx) * NZ + tz)

    def remote(src, dst, send, recv, device):
        return pltpu.make_async_remote_copy(
            src_ref=src, dst_ref=dst, send_sem=send, recv_sem=recv,
            device_id=device, device_id_type=MESH,
        )

    peers = [(ds, 0, 0, dz) for ds in range(SEG) for dz in range(NZ) if ds or dz]
    peers += [(0, 0, dx, 0) for dx in range(1, NX)]
    peers += [(ds, dy, 0, 0) for ds in range(SEG) for dy in range(1, NY)]
    barrier = pltpu.get_barrier_semaphore()
    for peer in peers:
        pl.semaphore_signal(barrier, inc=1, device_id=target(*peer), device_id_type=MESH)
    pl.semaphore_wait(barrier, len(peers))

    own_s = pltpu.make_async_copy(s_in.at[seg], s_all.at[seg, y, x, z], here.at[0])
    own_z = pltpu.make_async_copy(r_in.at[:, :, z], rz.at[z], here.at[1])
    own_s.start()
    own_z.start()
    s_z, r_z = [], []
    for ds in range(SEG):
        for dz in range(NZ):
            if ds or dz:
                k = ds * NZ + dz
                s_z.append(remote(s_in.at[lax.rem(seg + ds, SEG)], s_all.at[seg, y, x, z],
                                  sz_s.at[k], sz_r.at[k], target(ds, 0, 0, dz)))
    for dz in range(1, NZ):
        r_z.append(remote(r_in.at[:, :, lax.rem(z + dz, NZ)], rz.at[z],
                          rz_s.at[dz], rz_r.at[dz], target(0, 0, 0, dz)))
    for copy in s_z + r_z:
        copy.start()
    own_s.wait()
    for copy in s_z:
        copy.wait_recv()
    s_x = []
    for d in range(1, NX):
        s_x.append(remote(s_all.at[0, y, x], s_all.at[0, y, x],
                          sx_s.at[0, d], sx_r.at[0, d], target(0, 0, d, 0)))
        s_x.append(remote(s_all.at[1, y, x], s_all.at[1, y, x],
                          sx_s.at[1, d], sx_r.at[1, d], target(0, d, 0, 0)))
    for copy in s_x:
        copy.start()
    own_z.wait()
    for copy in r_z:
        copy.wait_recv()
    own_x = pltpu.make_async_copy(rz.at[:, :, x], rx.at[x], here.at[2])
    own_x.start()
    r_x = []
    for d in range(1, NX):
        r_x.append(remote(rz.at[:, :, lax.rem(x + d, NX)], rx.at[x],
                          rx_s.at[d], rx_r.at[d], target(0, 0, d, 0)))
    for copy in r_x:
        copy.start()
    for copy in s_x:
        copy.wait_recv()
    s_y = []
    for d in range(1, NY):
        s_y.append(remote(s_all.at[0, y], s_all.at[0, y],
                          sy_s.at[0, d], sy_r.at[0, d], target(0, d, 0, 0)))
        s_y.append(remote(s_all.at[1, :, x], s_all.at[1, :, x],
                          sy_s.at[1, d], sy_r.at[1, d], target(0, 0, d, 0)))
    for copy in s_y:
        copy.start()
    own_x.wait()
    for copy in r_x:
        copy.wait_recv()
    own_y = pltpu.make_async_copy(rx.at[:, :, y], r_fin.at[seg, y], here.at[3])
    own_y.start()
    r_y = []
    for ds in range(SEG):
        for d in range(NY):
            if ds or d:
                k = ds * NY + d
                r_y.append(remote(rx.at[:, :, lax.rem(y + d, NY)], r_fin.at[seg, y],
                                  ry_s.at[k], ry_r.at[k], target(ds, d, 0, 0)))
    for copy in r_y:
        copy.start()
    own_y.wait()
    for copy in s_y + r_y:
        copy.wait_recv()
    for copy in s_z + r_z + s_x + r_x + s_y + r_y:
        copy.wait_send()


def spread(s_loc, r_loc):
    vmem = pl.BlockSpec(memory_space=pltpu.VMEM)
    dma = pltpu.SemaphoreType.DMA
    return pl.pallas_call(
        spread_kernel,
        out_shape=(
            jax.ShapeDtypeStruct((SEG, NY, NX, NZ, 2 * SEQS, HALF), BF),
            jax.ShapeDtypeStruct((SEG, NY, NX, NZ, 1, LANES), F32),
        ),
        in_specs=[vmem, vmem],
        out_specs=(vmem, vmem),
        scratch_shapes=[
            pltpu.VMEM((NZ, NY, NX, 1, LANES), F32),
            pltpu.VMEM((NX, NZ, NY, 1, LANES), F32),
            dma((SEG * NZ,)), dma((SEG * NZ,)),
            dma((2, NX)), dma((2, NX)),
            dma((2, NY)), dma((2, NY)),
            dma((NZ,)), dma((NZ,)),
            dma((NX,)), dma((NX,)),
            dma((SEG * NY,)), dma((SEG * NY,)),
            dma((4,)),
        ],
        compiler_params=pltpu.CompilerParams(
            collective_id=0, has_side_effects=True, vmem_limit_bytes=24 << 20
        ),
        name="spread",
    )(s_loc, r_loc.reshape(NY, NX, NZ, 1, LANES))


VBLOCK = 32


def correlate_kernel(s_ref, r_ref, lag_ref, out_ref, flat, st, rt, cross):
    step = pl.program_id(0)

    @pl.when(step == 0)
    def _():
        shape = (LANES, LANES)
        eye = lax.broadcasted_iota(jnp.int32, shape, 0) == lax.broadcasted_iota(jnp.int32, shape, 1)
        eye = jnp.where(eye, 1.0, 0.0).astype(BF)
        for h in range(SEG):
            rt[h] = mm_nt(eye, r_ref[h].astype(BF))
            flat[...] = s_ref[h].reshape(CHIPS * 2 * SEQS, HALF).astype(F32)
            for g in range(2 * SEQS):
                piece = flat[pl.ds(g, CHIPS, stride=2 * SEQS), :].astype(BF)
                st[h, g] = mm_nt(eye, piece)

    for f in range(F_DEV):
        rr, ri = [], []
        for h in range(SEG):
            for m in range(M_DEV):
                g = (f * M_DEV + m) * 2
                rr.append(rt[h, RECS * g : RECS * (g + 1)])
                ri.append(rt[h, RECS * (g + 1) : RECS * (g + 2)])

        def body(b, carry, f=f, rr=rr, ri=ri):
            rows = pl.ds(pl.multiple_of(step * VBLOCK + b * 8, 8), 8)
            cr = jnp.zeros((8, RECS, LANES), F32)
            ci = jnp.zeros((8, RECS, LANES), F32)
            for h in range(SEG):
                for m in range(M_DEV):
                    g = (f * M_DEV + m) * 2
                    sr = st[h, g, rows, :][:, None, :]
                    si = st[h, g + 1, rows, :][:, None, :]
                    r, i = rr[h * M_DEV + m][None], ri[h * M_DEV + m][None]
                    cr = cr + sr * r + si * i
                    ci = ci + sr * i - si * r
            to = pl.ds(pl.multiple_of(b * 8 * RECS, 8 * RECS), 8 * RECS)
            cross[to, f * LANES : (f + 1) * LANES] = cr.reshape(8 * RECS, LANES).astype(BF)
            cross[to, NF + f * LANES : NF + (f + 1) * LANES] = (
                ci.reshape(8 * RECS, LANES).astype(BF)
            )
            return carry

        lax.fori_loop(0, VBLOCK // 8, body, 0, unroll=True)
    result = mm(cross[...], lag_ref[...]) * (1.0 / math.sqrt(MB * NF))
    out_ref[...] = result.astype(BF).reshape(VBLOCK, RECS, LAGS)


def correlate(s_all, r_all):
    return pl.pallas_call(
        correlate_kernel,
        out_shape=jax.ShapeDtypeStruct((HALF, RECS, LAGS), BF),
        grid=(HALF // VBLOCK,),
        in_specs=[
            pl.BlockSpec((SEG, CHIPS, 2 * SEQS, HALF), lambda k: (0, 0, 0, 0)),
            pl.BlockSpec((SEG, CHIPS, LANES), lambda k: (0, 0, 0)),
            pl.BlockSpec((2 * NF, LAGS), lambda k: (0, 0)),
        ],
        out_specs=pl.BlockSpec((VBLOCK, RECS, LAGS), lambda k: (k, 0, 0)),
        scratch_shapes=[
            pltpu.VMEM((CHIPS * 2 * SEQS, HALF), F32),
            pltpu.VMEM((SEG, 2 * SEQS, HALF, CHIPS), F32),
            pltpu.VMEM((SEG, LANES, CHIPS), F32),
            pltpu.VMEM((VBLOCK * RECS, 2 * NF), BF),
        ],
        compiler_params=pltpu.CompilerParams(vmem_limit_bytes=40 << 20),
        cost_estimate=pl.CostEstimate(flops=3 << 30, bytes_accessed=4 << 20, transcendentals=0),
        name="correlate",
    )(s_all, r_all, jnp.asarray(lag_table()))


def shards(records, fan_limit, sources):
    white = transform(records, jnp.asarray(time_table()))
    mixed = lax.all_to_all(white, "chan", split_axis=0, concat_axis=0, tiled=True)
    s_loc, r_loc = fan_filter(mixed, fan_limit, sources)
    s_all, r_all = spread(s_loc, r_loc)
    return correlate(
        s_all.reshape(SEG, CHIPS, 2 * SEQS, HALF), r_all.reshape(SEG, CHIPS, LANES)
    )


def solution(mesh):
    in_specs = (P(None, "chan", None), P(), P())
    out_specs = P("segment", "chan", None)
    return jax.shard_map(shards, mesh=mesh, in_specs=in_specs, out_specs=out_specs, check_vma=False)
```

```python
import functools
import math

import jax
import jax.numpy as jnp
import numpy as np
from jax import lax
from jax.experimental import pallas as pl
from jax.experimental.pallas import tpu as pltpu
from jax.sharding import PartitionSpec as P

NCH = 10240
NT = 7680
NF = 512
FLO = 32
NVS = 256
STRIDE = 10
LAGS = 512
MB = 4

epsilon = 1e-06

SEG = 2
NY, NX, NZ = 4, 4, 8
CHIPS = NY * NX * NZ
CH_DEV = NCH // CHIPS
F_DEV = NF // CHIPS
M_DEV = MB // SEG
SEQS = F_DEV * M_DEV
RECS = CH_DEV // STRIDE
HALF = NVS // SEG
LANES = 128
HALF_SEQS = SEQS // 2
WIDE = HALF_SEQS * CH_DEV
PLANE = NY * NX
RADIX = 4
STEPS = 3
QUARTER = NT // RADIX
KBLOCK = QUARTER // STEPS
ROWS = M_DEV * CH_DEV
MESH = pl.DeviceIdType.MESH
BF = jnp.bfloat16
F32 = jnp.float32


def as_bf16(array):
    return np.asarray(array, np.float32).astype(jnp.bfloat16)


def split(array):
    high = as_bf16(array)
    low = as_bf16(np.asarray(array, np.float64) - high.astype(np.float64))
    return high, low


def time_tables():
    plane, late = np.meshgrid(np.arange(PLANE), np.arange(NZ // RADIX))
    chips = plane * NZ + RADIX * late
    bins = FLO + CHIPS * np.arange(F_DEV)[:, None] + chips.reshape(1, -1)
    times = np.arange(QUARTER, dtype=np.int64)
    columns = []
    for residue in (0, 2, 1, 3):
        freqs = (bins + residue).reshape(-1)
        phase = freqs[:, None] * times[None, :] % NT
        angle = phase.astype(np.float32) * np.float32(2.0 * math.pi / NT)
        cosine, sine = np.cos(angle), np.sin(angle)
        columns.append(np.concatenate([cosine, -sine], axis=0))
        if residue % 2:
            turn = 1.0 if residue == 3 else -1.0
            columns.append(np.concatenate([turn * sine, turn * cosine], axis=0))
    table = np.stack(columns, axis=1).reshape(2 * CHIPS, 6, STEPS, KBLOCK)
    return as_bf16(table.transpose(2, 0, 1, 3).reshape(STEPS, 2 * CHIPS, 6 * KBLOCK))


def lag_table():
    lagged = np.arange(LAGS, dtype=np.int64) - LAGS // 2
    freqs = FLO + np.arange(NF, dtype=np.int64)
    phase = freqs[:, None] * lagged[None, :] % NT
    angle = phase.astype(np.float32) * np.float32(2.0 * math.pi / NT)
    return as_bf16(np.concatenate([np.cos(angle), -np.sin(angle)], axis=0))


def roots(rows, cols, modulus):
    phase = np.arange(rows)[:, None] * np.arange(cols)[None, :] % modulus
    angle = phase * (2.0 * math.pi / modulus)
    return np.cos(angle), -np.sin(angle)


def filter_tables():
    dr, di = roots(CHIPS, CHIPS, CHIPS)
    er = np.zeros((LANES, LANES))
    ei = np.zeros((LANES, LANES))
    er[:CH_DEV, :CH_DEV], ei[:CH_DEV, :CH_DEV] = roots(CH_DEV, CH_DEV, CH_DEV)
    tr = np.zeros((CHIPS, LANES))
    ti = np.zeros((CHIPS, LANES))
    tr[:, :CH_DEV], ti[:, :CH_DEV] = roots(CHIPS, CH_DEV, NCH)
    outer = np.block([[dr, -di], [di, dr]])
    inner = np.block([[er, ei], [-ei, er]])
    inner_back = np.block([[er, -ei], [ei, er]])
    outer_back = np.block([[dr, di], [-di, dr]])
    major = np.arange(CHIPS).reshape(PLANE, NZ).T.reshape(-1)
    outer_z = np.block([[dr[:, major], -di[:, major]], [di[:, major], dr[:, major]]])
    order = (outer, inner, inner_back, outer_back, outer_z)
    tables = np.stack([t for m in order for t in split(m)])
    twist = np.stack([tr, ti]).astype(np.float32)
    pick = np.zeros((2, SEQS, LANES, LANES), np.float32)
    for part in range(2):
        for q in range(SEQS):
            for u in range(RECS):
                pick[part, q, STRIDE * u, (q * 2 + part) * RECS + u] = 1.0
    return tables, twist, as_bf16(pick.reshape(2, SEQS * LANES, LANES))


def mm(left, right):
    return jnp.dot(left, right, preferred_element_type=F32)


def mm_nt(left, right):
    return lax.dot_general(left, right, (((1,), (1,)), ((), ())), preferred_element_type=F32)


def halves(value):
    high = value.astype(BF)
    return high, (value - high.astype(F32)).astype(BF)


def filter_half(h, x, column, limit_ref, tables, twist):
    tail = jnp.zeros((CHIPS, LANES // 2), BF)
    xs = jnp.concatenate(
        [
            jnp.concatenate([x[:, :WIDE], tail], axis=1),
            jnp.concatenate([x[:, WIDE:], tail], axis=1),
        ],
        axis=0,
    )
    outer = 0 if h == 0 else 8
    first = mm(tables[outer], xs) + mm(tables[outer + 1], xs)
    tr, ti = twist[0], twist[1]
    turned = []
    for q in range(HALF_SEQS):
        yr = first[:CHIPS, CH_DEV * q : CH_DEV * q + LANES]
        yi = first[CHIPS:, CH_DEV * q : CH_DEV * q + LANES]
        turned.append(jnp.concatenate([yr * tr - yi * ti, yr * ti + yi * tr], axis=1))
    high, low = halves(jnp.concatenate(turned, axis=0))
    wave = mm(high, tables[2]) + mm(high, tables[3]) + mm(low, tables[2])
    shape = (CHIPS, 2 * LANES)
    lane = lax.broadcasted_iota(jnp.int32, shape, 1) % LANES
    index = lax.broadcasted_iota(jnp.int32, shape, 0) + CHIPS * lane
    signed = jnp.where(index < NCH // 2, index, index - NCH)
    reach = jnp.where(index < NCH, jnp.abs(signed), NCH)
    kept = []
    for q in range(HALF_SEQS):
        limit = limit_ref[(2 * h + q // M_DEV) * CHIPS + column]
        kept.append(jnp.where(reach <= limit, wave[CHIPS * q : CHIPS * (q + 1)], 0.0))
    high, low = halves(jnp.concatenate(kept, axis=0))
    back = mm(high, tables[4]) + mm(high, tables[5]) + mm(low, tables[4])
    real, imag = [], []
    for q in range(HALF_SEQS):
        ur = back[CHIPS * q : CHIPS * (q + 1), :LANES]
        ui = back[CHIPS * q : CHIPS * (q + 1), LANES:]
        real.append(ur * tr + ui * ti)
        imag.append(ui * tr - ur * ti)
    high, low = halves(
        jnp.concatenate([jnp.concatenate(real, axis=1), jnp.concatenate(imag, axis=1)], axis=0)
    )
    field = mm(tables[6], high) + mm(tables[6], low) + mm(tables[7], high)
    return (field * (1.0 / NCH)).astype(BF)


def hot_sources(source):
    chip = ((source.astype(F32) + 0.5) * (1.0 / CH_DEV)).astype(jnp.int32)
    inside = source - CH_DEV * chip
    rows = lax.broadcasted_iota(jnp.int32, (LANES, NVS), 0)
    hot_inside = jnp.where(rows == inside, 1.0, 0.0).astype(BF)
    hot_chip = jnp.where(rows == chip, 1.0, 0.0)
    return hot_inside, hot_chip


def source_rows(field, hot_inside, hot_chip):
    lines = []
    for q in range(HALF_SEQS):
        for part in range(2):
            block = field[CHIPS * part : CHIPS * (part + 1), LANES * q : LANES * (q + 1)]
            chosen = mm(block, hot_inside) * hot_chip
            lines.append(jnp.sum(chosen, axis=0, keepdims=True))
    return lines


def reorder(new, old):
    rows = lax.broadcasted_iota(jnp.int32, (CHIPS, CHIPS), 0)
    cols = lax.broadcasted_iota(jnp.int32, (CHIPS, CHIPS), 1)
    return jnp.where(cols == old(*new(rows)), 1.0, 0.0).astype(BF)


def filtered_kernel(records, time_ref, limit_ref, src_ref, tables_hbm, twist_hbm, pick_hbm,
                    s_all, r_fin,
                    xbuf, tbuf, acc, tables, twist, pick,
                    a, g0, b0, x0, b1, g1, b2, x1, s_in, r_in, ry, rx,
                    in_sem, cz_s, cz_r, cp_s, cp_r, sz_s, sz_r, sx_s, sx_r, sy_s, sy_r,
                    ry_s, ry_r, rx_s, rx_r, rz_s, rz_r, here):
    seg = lax.axis_index("segment")
    chan = lax.axis_index("chan")
    z = lax.rem(chan, NZ)
    plane = lax.div(chan, NZ)
    x = lax.rem(plane, NX)
    y = lax.div(plane, NX)

    def zpeer(d, ds=0):
        return (lax.rem(seg + ds, SEG), plane * NZ + lax.rem(z + d, NZ))

    def ppeer(d):
        return (seg, lax.rem(plane + d, PLANE) * NZ + z)

    def xpeer(d):
        return (seg, (y * NX + lax.rem(x + d, NX)) * NZ + z)

    def ypeer(d):
        return (seg, (lax.rem(y + d, NY) * NX + x) * NZ + z)

    def remote(src, dst, send, recv, device):
        copy = pltpu.make_async_remote_copy(
            src_ref=src, dst_ref=dst, send_sem=send, recv_sem=recv,
            device_id=device, device_id_type=MESH,
        )
        copy.start()
        return copy

    def local(src, dst, sem):
        copy = pltpu.make_async_copy(src, dst, sem)
        copy.start()
        return copy

    loads = []
    for k in range(STEPS):
        row = []
        for s in range(RADIX):
            row.append(local(
                records.at[pl.ds(M_DEV * seg, M_DEV), :, pl.ds(QUARTER * s + KBLOCK * k, KBLOCK)],
                xbuf.at[k, s], in_sem.at[k, s]))
        row.append(local(time_ref.at[k], tbuf.at[k], in_sem.at[k, RADIX]))
        loads.append(row)
    later = [local(tables_hbm, tables, in_sem.at[STEPS, 0]),
             local(twist_hbm, twist, in_sem.at[STEPS, 1]),
             local(pick_hbm, pick, in_sem.at[STEPS, 2])]

    peers = [zpeer(d, ds) for ds in range(SEG) for d in range(NZ) if d or ds]
    peers += [ppeer(d) for d in range(1, PLANE)]
    barrier = pltpu.get_barrier_semaphore()
    for peer in peers:
        pl.semaphore_signal(barrier, inc=1, device_id=peer, device_id_type=MESH)

    for k in range(STEPS):
        for copy in loads[k]:
            copy.wait()
        q0, q1, q2, q3 = [xbuf[k, s].reshape(ROWS, KBLOCK).astype(F32) for s in range(RADIX)]
        s02, s13, d02, d13 = q0 + q2, q1 + q3, (q0 - q2).astype(BF), (q1 - q3).astype(BF)
        whole, rest = halves(s02 + s13)
        turn = (s02 - s13).astype(BF)

        def part(n):
            return tbuf[k, :, n * KBLOCK : (n + 1) * KBLOCK]

        sums = (
            mm_nt(part(0), whole) + mm_nt(part(0), rest),
            mm_nt(part(2), d02) + mm_nt(part(3), d13),
            mm_nt(part(1), turn),
            mm_nt(part(4), d02) + mm_nt(part(5), d13),
        )
        for r in range(RADIX):
            if k == 0:
                acc[r] = sums[r]
            else:
                acc[r] += sums[r]
    spectra = acc[...] * (1.0 / math.sqrt(NT))
    power = jnp.sum(jnp.sum(spectra * spectra, axis=0), axis=0, keepdims=True) * (1.0 / NF)
    white = spectra * lax.rsqrt(power + epsilon)[None]
    group = CHIPS // RADIX
    for h in range(2):
        for r in range(RADIX):
            blocks = []
            for part_of in range(2):
                for f in (2 * h, 2 * h + 1):
                    at = part_of * CHIPS + f * group
                    blocks.append(white[r, at : at + group])
            joined = jnp.concatenate(blocks, axis=1).astype(BF)
            a[h, 2 * r : 2 * r + 2] = joined.reshape(2, PLANE, 2 * WIDE)

    pl.semaphore_wait(barrier, len(peers))

    def slot(t):
        return lax.rem(t, RADIX) * 2 + lax.div(t, RADIX)

    z0 = [remote(a.at[0, slot(lax.rem(z + d, NZ))], g0.at[z], cz_s.at[0, d], cz_r.at[0, d], zpeer(d))
          for d in range(1, NZ)]
    own_z0 = local(a.at[0, slot(z)], g0.at[z], here.at[0])
    to_plane = reorder(lambda r: (r % NZ, r // NZ),
                       lambda t, p: ((t % RADIX) * 2 + t // RADIX) * PLANE + p)
    b1[...] = mm(to_plane, a[1].reshape(CHIPS, 2 * WIDE)).astype(BF).reshape(PLANE, NZ, 2 * WIDE)
    p1 = [remote(b1.at[lax.rem(plane + d, PLANE)], g1.at[plane], cp_s.at[1, d], cp_r.at[1, d], ppeer(d))
          for d in range(1, PLANE)]
    own_p1 = local(b1.at[plane], g1.at[plane], here.at[1])
    to_z = reorder(lambda r: (r % PLANE, r // PLANE), lambda p, t: p * NZ + t)
    own_p1.wait()
    for copy in p1:
        copy.wait_recv()
    b2[...] = mm(to_z, g1[...].reshape(CHIPS, 2 * WIDE)).astype(BF).reshape(NZ, PLANE, 2 * WIDE)
    z1 = [remote(b2.at[lax.rem(z + d, NZ)], x1.at[z], cz_s.at[1, d], cz_r.at[1, d], zpeer(d))
          for d in range(1, NZ)]
    own_z1 = local(b2.at[z], x1.at[z], here.at[2])
    from_z = reorder(lambda r: (r % NZ, r // NZ), lambda t, p: t * PLANE + p)
    own_z0.wait()
    for copy in z0:
        copy.wait_recv()
    b0[...] = mm(from_z, g0[...].reshape(CHIPS, 2 * WIDE)).astype(BF).reshape(PLANE, NZ, 2 * WIDE)
    p0 = [remote(b0.at[lax.rem(plane + d, PLANE)], x0.at[plane], cp_s.at[0, d], cp_r.at[0, d], ppeer(d))
          for d in range(1, PLANE)]
    own_p0 = local(b0.at[plane], x0.at[plane], here.at[3])
    for copy in later:
        copy.wait()
    hot_inside, hot_chip = hot_sources(src_ref[...])
    own_p0.wait()
    for copy in p0:
        copy.wait_recv()
    field = filter_half(0, x0[...].reshape(CHIPS, 2 * WIDE), chan, limit_ref, tables, twist)
    lines = source_rows(field, hot_inside, hot_chip)
    receivers = mm(field[:CHIPS], pick[0, 0]) + mm(field[CHIPS:], pick[1, 0])
    own_z1.wait()
    for copy in z1:
        copy.wait_recv()
    field = filter_half(1, x1[...].reshape(CHIPS, 2 * WIDE), chan, limit_ref, tables, twist)
    lines += source_rows(field, hot_inside, hot_chip)
    receivers += mm(field[:CHIPS], pick[0, 1]) + mm(field[CHIPS:], pick[1, 1])
    found = jnp.concatenate(lines, axis=0).astype(BF)
    s_in[0] = found[:, :HALF]
    s_in[1] = found[:, HALF:]

    own_s = local(s_in.at[seg], s_all.at[seg, y, x, z], here.at[4])
    s_z = [remote(s_in.at[lax.rem(seg + ds, SEG)], s_all.at[seg, y, x, z],
                  sz_s.at[ds, d], sz_r.at[ds, d], zpeer(d, ds))
           for ds in range(SEG) for d in range(NZ) if d or ds]
    r_in[...] = receivers.reshape(NY, NX, NZ, 1, LANES)
    r_y = [remote(r_in.at[lax.rem(y + d, NY)], ry.at[y], ry_s.at[d], ry_r.at[d], ypeer(d))
           for d in range(1, NY)]
    own_y = local(r_in.at[y], ry.at[y], here.at[5])
    own_s.wait()
    for copy in s_z:
        copy.wait_recv()
    s_x = []
    for d in range(1, NX):
        s_x.append(remote(s_all.at[0, y, x], s_all.at[0, y, x],
                          sx_s.at[0, d], sx_r.at[0, d], xpeer(d)))
        s_x.append(remote(s_all.at[1, y, x], s_all.at[1, y, x],
                          sx_s.at[1, d], sx_r.at[1, d], ypeer(d)))
    own_y.wait()
    for copy in r_y:
        copy.wait_recv()
    r_x = [remote(ry.at[:, lax.rem(x + d, NX)], rx.at[:, x], rx_s.at[d], rx_r.at[d], xpeer(d))
           for d in range(1, NX)]
    own_x = local(ry.at[:, x], rx.at[:, x], here.at[6])
    for copy in s_x:
        copy.wait_recv()

    def piece(part_of, at, n):
        if part_of == 0:
            return s_all.at[0, at, pl.ds(2 * n, 2)]
        return s_all.at[1, pl.ds(2 * n, 2), at]

    ends = ((y, ypeer, NY), (x, xpeer, NX))
    ahead, behind, onward = [], [], []
    for n in range(2):
        for part_of in range(2):
            me, peer, size = ends[part_of]
            up, down = piece(part_of, me, n), piece(part_of, me, 1 - n)
            ahead.append(remote(up, up, sy_s.at[part_of, 0, n], sy_r.at[part_of, 0, n], peer(1)))
            behind.append(remote(down, down, sy_s.at[part_of, 1, n], sy_r.at[part_of, 1, n],
                                 peer(size - 1)))
    own_x.wait()
    for copy in r_x:
        copy.wait_recv()
    r_z = [remote(rx.at[:, :, lax.rem(z + d, NZ)], r_fin.at[seg, :, :, z],
                  rz_s.at[ds, d], rz_r.at[ds, d], zpeer(d, ds))
           for ds in range(SEG) for d in range(NZ) if d or ds]
    own_r = local(rx.at[:, :, z], r_fin.at[seg, :, :, z], here.at[7])
    for part_of in range(2):
        me, peer, size = ends[part_of]
        ahead[part_of].wait_recv()
        got = piece(part_of, lax.rem(me + size - 1, size), 0)
        onward.append(remote(got, got, sy_s.at[part_of, 2, 0], sy_r.at[part_of, 2, 0], peer(1)))
        behind[part_of].wait_recv()
        got = piece(part_of, lax.rem(me + 1, size), 1)
        onward.append(remote(got, got, sy_s.at[part_of, 2, 1], sy_r.at[part_of, 2, 1],
                             peer(size - 1)))
    own_r.wait()
    for copy in ahead[2:] + behind[2:] + onward + r_z:
        copy.wait_recv()
    for copy in z0 + p1 + z1 + p0 + s_z + r_y + s_x + r_x + ahead + behind + onward + r_z:
        copy.wait_send()


def filtered(records, limits, sources):
    tables, twist, pick = filter_tables()
    hbm = pl.BlockSpec(memory_space=pl.ANY)
    smem = pl.BlockSpec(memory_space=pltpu.SMEM)
    vmem = pl.BlockSpec(memory_space=pltpu.VMEM)
    dma = pltpu.SemaphoreType.DMA
    by_z = pltpu.VMEM((NZ, PLANE, 2 * WIDE), BF)
    by_plane = pltpu.VMEM((PLANE, NZ, 2 * WIDE), BF)
    grid_of = pltpu.VMEM((NY, NX, NZ, 1, LANES), F32)
    pick = pick.reshape(2, 2, HALF_SEQS * LANES, LANES)
    return pl.pallas_call(
        filtered_kernel,
        out_shape=(
            jax.ShapeDtypeStruct((SEG, NY, NX, NZ, 2 * SEQS, HALF), BF),
            jax.ShapeDtypeStruct((SEG, NY, NX, NZ, 1, LANES), F32),
        ),
        in_specs=[hbm, hbm, smem, vmem, hbm, hbm, hbm],
        out_specs=(vmem, vmem),
        scratch_shapes=[
            pltpu.VMEM((STEPS, RADIX, M_DEV, CH_DEV, KBLOCK), BF),
            pltpu.VMEM((STEPS, 2 * CHIPS, 6 * KBLOCK), BF),
            pltpu.VMEM((RADIX, 2 * CHIPS, ROWS), F32),
            pltpu.VMEM(tables.shape, BF),
            pltpu.VMEM(twist.shape, F32),
            pltpu.VMEM(pick.shape, BF),
            pltpu.VMEM((2, NZ, PLANE, 2 * WIDE), BF),
            by_z, by_plane, by_plane, by_plane, by_plane, by_z, by_z,
            pltpu.VMEM((SEG, 2 * SEQS, HALF), BF),
            grid_of, grid_of, grid_of,
            dma((STEPS + 1, RADIX + 1)),
            dma((2, NZ)), dma((2, NZ)), dma((2, PLANE)), dma((2, PLANE)),
            dma((SEG, NZ)), dma((SEG, NZ)), dma((2, NX)), dma((2, NX)),
            dma((2, 3, 2)), dma((2, 3, 2)),
            dma((NY,)), dma((NY,)), dma((NX,)), dma((NX,)), dma((SEG, NZ)), dma((SEG, NZ)),
            dma((8,)),
        ],
        compiler_params=pltpu.CompilerParams(
            collective_id=0, has_side_effects=True, vmem_limit_bytes=56 << 20
        ),
        cost_estimate=pl.CostEstimate(flops=6 << 30, bytes_accessed=12 << 20, transcendentals=0),
        name="filtered",
    )(
        records,
        jnp.asarray(time_tables()),
        limits,
        sources.reshape(1, NVS),
        jnp.asarray(tables),
        jnp.asarray(twist),
        jnp.asarray(pick),
    )

VBLOCK = 32


def correlate_kernel(s_ref, r_ref, lag_ref, out_ref, flat, st, rt, cross):
    step = pl.program_id(0)

    @pl.when(step == 0)
    def _():
        shape = (LANES, LANES)
        eye = lax.broadcasted_iota(jnp.int32, shape, 0) == lax.broadcasted_iota(jnp.int32, shape, 1)
        eye = jnp.where(eye, 1.0, 0.0).astype(BF)
        for h in range(SEG):
            rt[h] = mm_nt(eye, r_ref[h].astype(BF))
            flat[...] = s_ref[h].reshape(CHIPS * 2 * SEQS, HALF).astype(F32)
            for g in range(2 * SEQS):
                piece = flat[pl.ds(g, CHIPS, stride=2 * SEQS), :].astype(BF)
                st[h, g] = mm_nt(eye, piece)

    for f in range(F_DEV):
        rr, ri = [], []
        for h in range(SEG):
            for m in range(M_DEV):
                g = (f * M_DEV + m) * 2
                rr.append(rt[h, RECS * g : RECS * (g + 1)])
                ri.append(rt[h, RECS * (g + 1) : RECS * (g + 2)])

        def body(b, carry, f=f, rr=rr, ri=ri):
            rows = pl.ds(pl.multiple_of(step * VBLOCK + b * 8, 8), 8)
            cr = jnp.zeros((8, RECS, LANES), F32)
            ci = jnp.zeros((8, RECS, LANES), F32)
            for h in range(SEG):
                for m in range(M_DEV):
                    g = (f * M_DEV + m) * 2
                    sr = st[h, g, rows, :][:, None, :]
                    si = st[h, g + 1, rows, :][:, None, :]
                    r, i = rr[h * M_DEV + m][None], ri[h * M_DEV + m][None]
                    cr = cr + sr * r + si * i
                    ci = ci + sr * i - si * r
            to = pl.ds(pl.multiple_of(b * 8 * RECS, 8 * RECS), 8 * RECS)
            cross[to, f * LANES : (f + 1) * LANES] = cr.reshape(8 * RECS, LANES).astype(BF)
            cross[to, NF + f * LANES : NF + (f + 1) * LANES] = (
                ci.reshape(8 * RECS, LANES).astype(BF)
            )
            return carry

        lax.fori_loop(0, VBLOCK // 8, body, 0, unroll=True)
    result = mm(cross[...], lag_ref[...]) * (1.0 / math.sqrt(MB * NF))
    out_ref[...] = result.astype(BF).reshape(VBLOCK, RECS, LAGS)


def correlate(s_all, r_all):
    return pl.pallas_call(
        correlate_kernel,
        out_shape=jax.ShapeDtypeStruct((HALF, RECS, LAGS), BF),
        grid=(HALF // VBLOCK,),
        in_specs=[
            pl.BlockSpec((SEG, CHIPS, 2 * SEQS, HALF), lambda k: (0, 0, 0, 0)),
            pl.BlockSpec((SEG, CHIPS, LANES), lambda k: (0, 0, 0)),
            pl.BlockSpec((2 * NF, LAGS), lambda k: (0, 0)),
        ],
        out_specs=pl.BlockSpec((VBLOCK, RECS, LAGS), lambda k: (k, 0, 0)),
        scratch_shapes=[
            pltpu.VMEM((CHIPS * 2 * SEQS, HALF), F32),
            pltpu.VMEM((SEG, 2 * SEQS, HALF, CHIPS), F32),
            pltpu.VMEM((SEG, LANES, CHIPS), F32),
            pltpu.VMEM((VBLOCK * RECS, 2 * NF), BF),
        ],
        compiler_params=pltpu.CompilerParams(vmem_limit_bytes=40 << 20),
        cost_estimate=pl.CostEstimate(flops=3 << 30, bytes_accessed=4 << 20, transcendentals=0),
        name="correlate",
    )(s_all, r_all, jnp.asarray(lag_table()))


def shards(records, fan_limit, sources):
    s_all, r_all = filtered(records, fan_limit, sources)
    return correlate(
        s_all.reshape(SEG, CHIPS, 2 * SEQS, HALF), r_all.reshape(SEG, CHIPS, LANES)
    )


def solution(mesh):
    in_specs = (P(None, "chan", None), P(), P())
    out_specs = P("segment", "chan", None)
    return jax.shard_map(shards, mesh=mesh, in_specs=in_specs, out_specs=out_specs, check_vma=False)
```

```python
import functools
import math

import jax
import jax.numpy as jnp
import numpy as np
from jax import lax
from jax.experimental import pallas as pl
from jax.experimental.pallas import tpu as pltpu
from jax.sharding import PartitionSpec as P

NCH = 10240
NT = 7680
NF = 512
FLO = 32
NVS = 256
STRIDE = 10
LAGS = 512
MB = 4

epsilon = 1e-06

SEG = 2
NY, NX, NZ = 4, 4, 8
CHIPS = NY * NX * NZ
CH_DEV = NCH // CHIPS
F_DEV = NF // CHIPS
M_DEV = MB // SEG
SEQS = F_DEV * M_DEV
RECS = CH_DEV // STRIDE
VBLOCK = 32
HALF = NVS // SEG
LANES = 128
HALF_SEQS = SEQS // 2
WIDE = HALF_SEQS * CH_DEV
PLANE = NY * NX
RADIX = 4
STEPS = 5
QUARTER = NT // RADIX
KBLOCK = QUARTER // STEPS
ROWS = M_DEV * CH_DEV
MESH = pl.DeviceIdType.MESH
FAR_Z = sorted(range(1, NZ), key=lambda d: -min(d, NZ - d))
FAR_PLANE = sorted(
    range(1, NY * NX), key=lambda d: -min(d // NX, NY - d // NX) - min(d % NX, NX - d % NX)
)
BF = jnp.bfloat16
F32 = jnp.float32


def as_bf16(array):
    return np.asarray(array, np.float32).astype(jnp.bfloat16)


def split(array):
    high = as_bf16(array)
    low = as_bf16(np.asarray(array, np.float64) - high.astype(np.float64))
    return high, low


def time_tables():
    plane, late = np.meshgrid(np.arange(PLANE), np.arange(NZ // RADIX))
    chips = plane * NZ + RADIX * late
    bins = FLO + CHIPS * np.arange(F_DEV)[:, None] + chips.reshape(1, -1)
    times = np.arange(QUARTER, dtype=np.int64)
    tables = []
    for residue in range(RADIX):
        freqs = (bins + residue).reshape(-1)
        phase = times[:, None] * freqs[None, :] % NT
        angle = phase.astype(np.float32) * np.float32(2.0 * math.pi / NT)
        tables.append(np.concatenate([np.cos(angle), -np.sin(angle)], axis=1))
    table = np.stack(tables).reshape(RADIX, STEPS, KBLOCK, 2 * CHIPS)
    return as_bf16(table.transpose(1, 0, 2, 3))


def lag_table():
    lagged = np.arange(LAGS, dtype=np.int64) - LAGS // 2
    freqs = FLO + np.arange(NF, dtype=np.int64)
    phase = freqs[:, None] * lagged[None, :] % NT
    angle = phase.astype(np.float32) * np.float32(2.0 * math.pi / NT)
    return as_bf16(np.stack([np.cos(angle), -np.sin(angle)]).reshape(2, 2, NF // 2, LAGS)
                   .transpose(1, 0, 2, 3).reshape(2, NF, LAGS))


def roots(rows, cols, modulus):
    phase = np.arange(rows)[:, None] * np.arange(cols)[None, :] % modulus
    angle = phase * (2.0 * math.pi / modulus)
    return np.cos(angle), -np.sin(angle)


def filter_tables():
    dr, di = roots(CHIPS, CHIPS, CHIPS)
    er = np.zeros((LANES, LANES))
    ei = np.zeros((LANES, LANES))
    er[:CH_DEV, :CH_DEV], ei[:CH_DEV, :CH_DEV] = roots(CH_DEV, CH_DEV, CH_DEV)
    tr = np.zeros((CHIPS, LANES))
    ti = np.zeros((CHIPS, LANES))
    tr[:, :CH_DEV], ti[:, :CH_DEV] = roots(CHIPS, CH_DEV, NCH)
    outer = np.block([[dr, -di], [di, dr]])
    inner = np.block([[er, ei], [-ei, er]])
    inner_back = np.block([[er, -ei], [ei, er]])
    outer_back = np.block([[dr, di], [-di, dr]])
    major = np.arange(CHIPS).reshape(PLANE, NZ).T.reshape(-1)
    outer_z = np.block([[dr[:, major], -di[:, major]], [di[:, major], dr[:, major]]])
    order = (outer, inner, inner_back, outer_back, outer_z)
    tables = np.stack([t for m in order for t in split(m)])
    twist = np.stack([tr, ti]).astype(np.float32)
    pick = np.zeros((2, SEQS, LANES, LANES), np.float32)
    for part in range(2):
        for q in range(SEQS):
            for u in range(RECS):
                pick[part, q, STRIDE * u, (q * 2 + part) * RECS + u] = 1.0
    return tables, twist, as_bf16(pick.reshape(2, SEQS * LANES, LANES))


def mm(left, right):
    return jnp.dot(left, right, preferred_element_type=F32)


def mm_nt(left, right):
    return lax.dot_general(left, right, (((1,), (1,)), ((), ())), preferred_element_type=F32)


def halves(value):
    high = value.astype(BF)
    return high, (value - high.astype(F32)).astype(BF)


def filter_half(h, x, column, limit_ref, tables, twist):
    tail = jnp.zeros((CHIPS, LANES // 2), BF)
    xs = jnp.concatenate(
        [
            jnp.concatenate([x[:, :WIDE], tail], axis=1),
            jnp.concatenate([x[:, WIDE:], tail], axis=1),
        ],
        axis=0,
    )
    outer = 0 if h == 0 else 8
    first = mm(tables[outer], xs) + mm(tables[outer + 1], xs)
    tr, ti = twist[0], twist[1]
    turned = []
    for q in range(HALF_SEQS):
        yr = first[:CHIPS, CH_DEV * q : CH_DEV * q + LANES]
        yi = first[CHIPS:, CH_DEV * q : CH_DEV * q + LANES]
        turned.append(jnp.concatenate([yr * tr - yi * ti, yr * ti + yi * tr], axis=1))
    high, low = halves(jnp.concatenate(turned, axis=0))
    wave = mm(high, tables[2]) + mm(high, tables[3]) + mm(low, tables[2])
    shape = (CHIPS, 2 * LANES)
    lane = lax.broadcasted_iota(jnp.int32, shape, 1) % LANES
    index = lax.broadcasted_iota(jnp.int32, shape, 0) + CHIPS * lane
    signed = jnp.where(index < NCH // 2, index, index - NCH)
    reach = jnp.where(index < NCH, jnp.abs(signed), NCH)
    kept = []
    for q in range(HALF_SEQS):
        limit = limit_ref[0, (2 * h + q // M_DEV) * CHIPS + column]
        kept.append(jnp.where(reach <= limit, wave[CHIPS * q : CHIPS * (q + 1)], 0.0))
    high, low = halves(jnp.concatenate(kept, axis=0))
    back = mm(high, tables[4]) + mm(high, tables[5]) + mm(low, tables[4])
    real, imag = [], []
    for q in range(HALF_SEQS):
        ur = back[CHIPS * q : CHIPS * (q + 1), :LANES]
        ui = back[CHIPS * q : CHIPS * (q + 1), LANES:]
        real.append(ur * tr + ui * ti)
        imag.append(ui * tr - ur * ti)
    high, low = halves(
        jnp.concatenate([jnp.concatenate(real, axis=1), jnp.concatenate(imag, axis=1)], axis=0)
    )
    field = mm(tables[6], high) + mm(tables[6], low) + mm(tables[7], high)
    return (field * (1.0 / NCH)).astype(BF)


def hot_sources(source):
    chip = ((source.astype(F32) + 0.5) * (1.0 / CH_DEV)).astype(jnp.int32)
    inside = source - CH_DEV * chip
    rows = lax.broadcasted_iota(jnp.int32, (LANES, NVS), 0)
    hot_inside = jnp.where(rows == inside, 1.0, 0.0).astype(BF)
    hot_chip = jnp.where(rows == chip, 1.0, 0.0)
    return hot_inside, hot_chip


def source_rows(field, hot_inside, hot_chip):
    lines = []
    for q in range(HALF_SEQS):
        for part in range(2):
            block = field[CHIPS * part : CHIPS * (part + 1), LANES * q : LANES * (q + 1)]
            chosen = mm(block, hot_inside) * hot_chip
            lines.append(jnp.sum(chosen, axis=0, keepdims=True))
    return jnp.concatenate(lines, axis=0).astype(BF)


def reorder(new, old):
    rows = lax.broadcasted_iota(jnp.int32, (CHIPS, CHIPS), 0)
    cols = lax.broadcasted_iota(jnp.int32, (CHIPS, CHIPS), 1)
    return jnp.where(cols == old(*new(rows)), 1.0, 0.0).astype(BF)


def sources_across(h, s_all, flat, st, eye):
    lines = 2 * HALF_SEQS
    for g in range(SEG):
        flat[...] = s_all[h, g].reshape(CHIPS * lines, HALF).astype(F32)
        for n in range(lines):
            st[g, n] = mm_nt(eye, flat[pl.ds(n, CHIPS, stride=lines), :].astype(BF))


def correlate_half(h, st, rt, lag, cross, total, keep):
    blocks = HALF // VBLOCK

    def spread_block(b):
        for f in range(F_DEV // 2):
            rr, ri = [], []
            for g in range(SEG):
                for m in range(M_DEV):
                    at = (((2 * h + f) * M_DEV + m) * 2) * RECS
                    rr.append(rt[g, at : at + RECS])
                    ri.append(rt[g, at + RECS : at + 2 * RECS])
            for v in range(VBLOCK // 8):
                rows = slice(b * VBLOCK + v * 8, b * VBLOCK + v * 8 + 8)
                cr = jnp.zeros((8, RECS, LANES), F32)
                ci = jnp.zeros((8, RECS, LANES), F32)
                for g in range(SEG):
                    for m in range(M_DEV):
                        n = (f * M_DEV + m) * 2
                        sr = st[g, n, rows, :][:, None, :]
                        si = st[g, n + 1, rows, :][:, None, :]
                        r, i = rr[g * M_DEV + m][None], ri[g * M_DEV + m][None]
                        cr = cr + sr * r + si * i
                        ci = ci + sr * i - si * r
                to = slice(v * 8 * RECS, (v + 1) * 8 * RECS)
                cross[b, to, f * LANES : (f + 1) * LANES] = cr.reshape(8 * RECS, LANES).astype(BF)
                cross[b, to, NF // 2 + f * LANES : NF // 2 + (f + 1) * LANES] = (
                    ci.reshape(8 * RECS, LANES).astype(BF)
                )

    def lag_block(b):
        result = mm(cross[b], lag[h])
        if h == 0:
            total[b] = result
        else:
            keep(b, (result + total[b]) * (1.0 / math.sqrt(MB * NF)))

    for b in range(blocks):
        spread_block(b)
        if b:
            lag_block(b - 1)
    lag_block(blocks - 1)


def whole_kernel(records, time_ref, limit_hbm, src_hbm, tables_hbm, twist_hbm, pick_hbm,
                    lag_hbm, out_ref, s_all, r_fin, flat, st, rt, cross, total, lag,
                    limit_ref, src_ref, result_buf,
                    xbuf, tbuf, acc, tables, twist, pick,
                    a, g0, b0, x0, b1, g1, b2, x1, s_in, r_in, ry, rx,
                    in_sem, cz_s, cz_r, cp_s, cp_r, sz_s, sz_r, sx_s, sx_r,
                    ry_s, ry_r, rx_s, rx_r, rz_s, rz_r, here):
    seg = lax.axis_index("segment")
    chan = lax.axis_index("chan")
    z = lax.rem(chan, NZ)
    plane = lax.div(chan, NZ)
    x = lax.rem(plane, NX)
    y = lax.div(plane, NX)

    def zpeer(d, ds=0):
        return (lax.rem(seg + ds, SEG), plane * NZ + lax.rem(z + d, NZ))

    def ppeer(d):
        return (seg, lax.rem(plane + d, PLANE) * NZ + z)

    def xpeer(d):
        return (seg, (y * NX + lax.rem(x + d, NX)) * NZ + z)

    def ypeer(d):
        return (seg, (lax.rem(y + d, NY) * NX + x) * NZ + z)

    def remote(src, dst, send, recv, device):
        copy = pltpu.make_async_remote_copy(
            src_ref=src, dst_ref=dst, send_sem=send, recv_sem=recv,
            device_id=device, device_id_type=MESH,
        )
        copy.start()
        return copy

    def local(src, dst, sem):
        copy = pltpu.make_async_copy(src, dst, sem)
        copy.start()
        return copy

    loads = [local(records.at[pl.ds(M_DEV * seg, M_DEV), :, pl.ds(QUARTER * s, QUARTER)],
                   xbuf.at[s], in_sem.at[0, s]) for s in range(RADIX)]
    chunks = [local(time_ref.at[k], tbuf.at[k], in_sem.at[1, k]) for k in range(2)]

    peers = [zpeer(d, ds) for ds in range(SEG) for d in range(NZ) if d or ds]
    peers += [ppeer(d) for d in range(1, PLANE)]
    barrier = pltpu.get_barrier_semaphore()
    for peer in peers:
        pl.semaphore_signal(barrier, inc=1, device_id=peer, device_id_type=MESH)
    chunks += [local(time_ref.at[k], tbuf.at[k], in_sem.at[1, k]) for k in range(2, STEPS)]
    later = [local(tables_hbm, tables, in_sem.at[2, 0]), local(twist_hbm, twist, in_sem.at[2, 1]),
             local(pick_hbm, pick, in_sem.at[2, 2]), local(limit_hbm, limit_ref, in_sem.at[0, 4]),
             local(src_hbm, src_ref, in_sem.at[2, 4])]
    lag_load = local(lag_hbm, lag, in_sem.at[2, 3])
    for copy in loads:
        copy.wait()

    for k in range(STEPS):
        chunks[k].wait()
        q0, q1, q2, q3 = [
            xbuf[s, :, :, k * KBLOCK : (k + 1) * KBLOCK].reshape(ROWS, KBLOCK).astype(F32)
            for s in range(RADIX)
        ]
        s02, s13, d02, d13 = q0 + q2, q1 + q3, (q0 - q2).astype(BF), (q1 - q3).astype(BF)
        whole, rest = halves(s02 + s13)
        turn = (s02 - s13).astype(BF)
        sums = (
            mm(whole, tbuf[k, 0]) + mm(rest, tbuf[k, 0]),
            mm(turn, tbuf[k, 2]),
            mm(d02, tbuf[k, 1]),
            mm(d13, tbuf[k, 1]),
            mm(d02, tbuf[k, 3]),
            mm(d13, tbuf[k, 3]),
        )
        for n in range(6):
            if k == 0:
                acc[n] = sums[n]
            else:
                acc[n] += sums[n]

    def turned_by(n, sign):
        real = acc[n, :, :CHIPS] + sign * acc[n + 1, :, CHIPS:]
        imag = acc[n, :, CHIPS:] - sign * acc[n + 1, :, :CHIPS]
        return jnp.concatenate([real, imag], axis=1)

    scale = 1.0 / math.sqrt(NT)
    spectra = [v * scale for v in (acc[0], turned_by(2, 1.0), acc[1], turned_by(4, -1.0))]
    squares = sum(v * v for v in spectra)
    power = jnp.sum(squares, axis=1, keepdims=True) * (1.0 / NF)
    factor = lax.rsqrt(power + epsilon)
    rows = lax.broadcasted_iota(jnp.int32, (2 * CHIPS, 2 * CHIPS), 0)
    cols = lax.broadcasted_iota(jnp.int32, (2 * CHIPS, 2 * CHIPS), 1)
    eye = jnp.where(rows == cols, 1.0, 0.0).astype(BF)
    white = [mm_nt(eye, (v * factor).astype(BF)) for v in spectra]
    group = CHIPS // RADIX
    for h in range(2):
        for r in range(RADIX):
            blocks = []
            for part_of in range(2):
                for f in (2 * h, 2 * h + 1):
                    at = part_of * CHIPS + f * group
                    blocks.append(white[r][at : at + group])
            joined = jnp.concatenate(blocks, axis=1).astype(BF)
            a[h, 2 * r : 2 * r + 2] = joined.reshape(2, PLANE, 2 * WIDE)

    pl.semaphore_wait(barrier, len(peers))

    def slot(t):
        return lax.rem(t, RADIX) * 2 + lax.div(t, RADIX)

    z0 = [remote(a.at[0, slot(lax.rem(z + d, NZ))], g0.at[z], cz_s.at[0, d], cz_r.at[0, d], zpeer(d))
          for d in FAR_Z]
    own_z0 = local(a.at[0, slot(z)], g0.at[z], here.at[0])
    to_plane = reorder(lambda r: (r % NZ, r // NZ),
                       lambda t, p: ((t % RADIX) * 2 + t // RADIX) * PLANE + p)
    b1[...] = mm(to_plane, a[1].reshape(CHIPS, 2 * WIDE)).astype(BF).reshape(PLANE, NZ, 2 * WIDE)
    p1 = [remote(b1.at[lax.rem(plane + d, PLANE)], g1.at[plane], cp_s.at[1, d], cp_r.at[1, d], ppeer(d))
          for d in FAR_PLANE]
    own_p1 = local(b1.at[plane], g1.at[plane], here.at[1])
    to_z = reorder(lambda r: (r % PLANE, r // PLANE), lambda p, t: p * NZ + t)
    own_p1.wait()
    for copy in p1:
        copy.wait_recv()
    b2[...] = mm(to_z, g1[...].reshape(CHIPS, 2 * WIDE)).astype(BF).reshape(NZ, PLANE, 2 * WIDE)
    z1 = [remote(b2.at[lax.rem(z + d, NZ)], x1.at[z], cz_s.at[1, d], cz_r.at[1, d], zpeer(d))
          for d in FAR_Z]
    own_z1 = local(b2.at[z], x1.at[z], here.at[2])
    from_z = reorder(lambda r: (r % NZ, r // NZ), lambda t, p: t * PLANE + p)
    own_z0.wait()
    for copy in z0:
        copy.wait_recv()
    b0[...] = mm(from_z, g0[...].reshape(CHIPS, 2 * WIDE)).astype(BF).reshape(PLANE, NZ, 2 * WIDE)
    p0 = [remote(b0.at[lax.rem(plane + d, PLANE)], x0.at[plane], cp_s.at[0, d], cp_r.at[0, d], ppeer(d))
          for d in FAR_PLANE]
    own_p0 = local(b0.at[plane], x0.at[plane], here.at[3])
    for copy in later:
        copy.wait()
    hot_inside, hot_chip = hot_sources(src_ref[...])
    own_p0.wait()
    for copy in p0:
        copy.wait_recv()
    field = filter_half(0, x0[...].reshape(CHIPS, 2 * WIDE), chan, limit_ref, tables, twist)
    receivers = mm(field[:CHIPS], pick[0, 0]) + mm(field[CHIPS:], pick[1, 0])
    found = source_rows(field, hot_inside, hot_chip)
    s_in[0, 0] = found[:, :HALF]
    s_in[0, 1] = found[:, HALF:]

    def send_z(h):
        sent = [remote(s_in.at[h, lax.rem(seg + ds, SEG)], s_all.at[h, seg, y, x, z],
                       sz_s.at[h, ds, d], sz_r.at[h, ds, d], zpeer(d, ds))
                for d in FAR_Z + [0] for ds in range(SEG) if d or ds]
        return sent, local(s_in.at[h, seg], s_all.at[h, seg, y, x, z], here.at[4 + h])

    first_axis, second_axis = (xpeer, ypeer), (ypeer, xpeer)

    def block(h, p, d, e):
        if p == 0:
            return s_all.at[h, 0, lax.rem(y + e, NY), lax.rem(x + NX - d, NX)]
        return s_all.at[h, 1, lax.rem(y + NY - d, NY), lax.rem(x + e, NX)]

    def send_block(h, p, d, e, kind, device):
        one = block(h, p, d, e)
        return remote(one, one, sx_s.at[h, p, kind, d], sx_r.at[h, p, kind, d], device)

    def phase_own(h):
        along = [None] * 4
        for d in (2, 1, 3):
            along[d] = [remote(block(h, p, 0, 0), block(h, p, 0, 0), sx_s.at[h, p, 0, d],
                               sx_r.at[h, p, 0, d], first_axis[p](d)) for p in range(2)]
        up = [None] * 4
        down = [None] * 4
        up[0] = [send_block(h, p, 0, 0, 1, second_axis[p](1)) for p in range(2)]
        down[0] = [send_block(h, p, 0, 0, 2, second_axis[p](3)) for p in range(2)]
        return along, up, down

    def phase_across(h, along, up, down):
        for d in (1, 3, 2):
            up[d], down[d] = [], []
            for p in range(2):
                along[d][p].wait_recv()
                up[d].append(send_block(h, p, d, 0, 1, second_axis[p](1)))
                down[d].append(send_block(h, p, d, 0, 2, second_axis[p](3)))

    def phase_relay(h, up, down):
        relay = [None] * 4
        for d in (0, 1, 3, 2):
            relay[d] = []
            for p in range(2):
                if d % 2 == 0:
                    up[d][p].wait_recv()
                    relay[d].append(send_block(h, p, d, 3, 3, second_axis[p](1)))
                else:
                    down[d][p].wait_recv()
                    relay[d].append(send_block(h, p, d, 1, 3, second_axis[p](3)))
        return relay

    def phase_done(up, down, relay):
        for d in range(4):
            for p in range(2):
                (down if d % 2 == 0 else up)[d][p].wait_recv()
                relay[d][p].wait_recv()

    s_z0, own_s0 = send_z(0)
    own_z1.wait()
    for copy in z1:
        copy.wait_recv()
    field = filter_half(1, x1[...].reshape(CHIPS, 2 * WIDE), chan, limit_ref, tables, twist)
    found = source_rows(field, hot_inside, hot_chip)
    s_in[1, 0] = found[:, :HALF]
    s_in[1, 1] = found[:, HALF:]
    s_z1, own_s1 = send_z(1)
    receivers += mm(field[:CHIPS], pick[0, 1]) + mm(field[CHIPS:], pick[1, 1])
    r_in[...] = receivers.reshape(NY, NX, NZ, 1, LANES)
    r_y = [remote(r_in.at[lax.rem(y + d, NY)], ry.at[y], ry_s.at[d], ry_r.at[d], ypeer(d))
           for d in range(1, NY)]
    own_y = local(r_in.at[y], ry.at[y], here.at[6])
    own_s0.wait()
    for copy in s_z0:
        copy.wait_recv()
    along0, up0, down0 = phase_own(0)
    for copy in z0 + p1 + z1 + p0:
        copy.wait_send()
    own_y.wait()
    for copy in r_y:
        copy.wait_recv()
    r_x = [remote(ry.at[:, lax.rem(x + d, NX)], rx.at[:, x], rx_s.at[d], rx_r.at[d], xpeer(d))
           for d in range(1, NX)]
    own_x = local(ry.at[:, x], rx.at[:, x], here.at[7])
    phase_across(0, along0, up0, down0)
    own_s1.wait()
    for copy in s_z1:
        copy.wait_recv()
    along1, up1, down1 = phase_own(1)
    own_x.wait()
    for copy in r_x:
        copy.wait_recv()
    r_z = [remote(rx.at[:, :, lax.rem(z + d, NZ)], r_fin.at[seg, :, :, z],
                  rz_s.at[ds, d], rz_r.at[ds, d], zpeer(d, ds))
           for d in FAR_Z + [0] for ds in range(SEG) if d or ds]
    own_r = local(rx.at[:, :, z], r_fin.at[seg, :, :, z], here.at[8])
    relay0 = phase_relay(0, up0, down0)
    for copy in s_z0 + s_z1 + r_y + r_x:
        copy.wait_send()
    phase_across(1, along1, up1, down1)
    phase_done(up0, down0, relay0)
    small = eye[:LANES, :LANES]
    sources_across(0, s_all, flat, st, small)
    relay1 = phase_relay(1, up1, down1)
    own_r.wait()
    for copy in r_z:
        copy.wait_recv()
    for g in range(SEG):
        rt[g] = mm_nt(small, r_fin[g].reshape(CHIPS, LANES).astype(BF))
    lag_load.wait()
    correlate_half(0, st, rt, lag, cross, total, None)
    for copy in r_z:
        copy.wait_send()
    for row in along0[1:] + along1[1:] + up0 + down0 + relay0:
        for copy in row:
            copy.wait_send()
    phase_done(up1, down1, relay1)
    sources_across(1, s_all, flat, st, small)
    writes = []

    def keep(b, result):
        part = slice(b * VBLOCK, (b + 1) * VBLOCK)
        result_buf[part] = result.astype(BF).reshape(VBLOCK, RECS, LAGS)
        at = pl.ds(b * VBLOCK, VBLOCK)
        writes.append(local(result_buf.at[at], out_ref.at[at], here.at[9 + b]))

    correlate_half(1, st, rt, lag, cross, total, keep)
    for row in up1 + down1 + relay1:
        for copy in row:
            copy.wait_send()
    for copy in writes:
        copy.wait()


def correlations(records, limits, sources):
    tables, twist, pick = filter_tables()
    hbm = pl.BlockSpec(memory_space=pl.ANY)
    dma = pltpu.SemaphoreType.DMA
    by_z = pltpu.VMEM((NZ, PLANE, 2 * WIDE), BF)
    by_plane = pltpu.VMEM((PLANE, NZ, 2 * WIDE), BF)
    grid_of = pltpu.VMEM((NY, NX, NZ, 1, LANES), F32)
    pick = pick.reshape(2, 2, HALF_SEQS * LANES, LANES)
    return pl.pallas_call(
        whole_kernel,
        out_shape=jax.ShapeDtypeStruct((HALF, RECS, LAGS), BF),
        in_specs=[hbm] * 8,
        out_specs=hbm,
        scratch_shapes=[
            pltpu.VMEM((2, SEG, NY, NX, NZ, SEQS, HALF), BF),
            pltpu.VMEM((SEG, NY, NX, NZ, 1, LANES), F32),
            pltpu.VMEM((CHIPS * SEQS, HALF), F32),
            pltpu.VMEM((SEG, SEQS, HALF, CHIPS), F32),
            pltpu.VMEM((SEG, LANES, CHIPS), F32),
            pltpu.VMEM((HALF // VBLOCK, VBLOCK * RECS, NF), BF),
            pltpu.VMEM((HALF // VBLOCK, VBLOCK * RECS, LAGS), F32),
            pltpu.VMEM((2, NF, LAGS), BF),
            pltpu.SMEM((1, NF), jnp.int32),
            pltpu.VMEM((1, NVS), jnp.int32),
            pltpu.VMEM((HALF, RECS, LAGS), BF),
            pltpu.VMEM((RADIX, M_DEV, CH_DEV, QUARTER), BF),
            pltpu.VMEM((STEPS, RADIX, KBLOCK, 2 * CHIPS), BF),
            pltpu.VMEM((6, ROWS, 2 * CHIPS), F32),
            pltpu.VMEM(tables.shape, BF),
            pltpu.VMEM(twist.shape, F32),
            pltpu.VMEM(pick.shape, BF),
            pltpu.VMEM((2, NZ, PLANE, 2 * WIDE), BF),
            by_z, by_plane, by_plane, by_plane, by_plane, by_z, by_z,
            pltpu.VMEM((2, SEG, SEQS, HALF), BF),
            grid_of, grid_of, grid_of,
            dma((3, STEPS)),
            dma((2, NZ)), dma((2, NZ)), dma((2, PLANE)), dma((2, PLANE)),
            dma((2, SEG, NZ)), dma((2, SEG, NZ)), dma((2, 2, 4, NX)), dma((2, 2, 4, NX)),
            dma((NY,)), dma((NY,)), dma((NX,)), dma((NX,)), dma((SEG, NZ)), dma((SEG, NZ)),
            dma((9 + HALF // VBLOCK,)),
        ],
        compiler_params=pltpu.CompilerParams(
            collective_id=0, has_side_effects=True, vmem_limit_bytes=57 << 20
        ),
        cost_estimate=pl.CostEstimate(flops=6 << 30, bytes_accessed=12 << 20, transcendentals=0),
        name="correlations",
    )(
        records,
        jnp.asarray(time_tables()),
        limits.reshape(1, NF),
        sources.reshape(1, NVS),
        jnp.asarray(tables),
        jnp.asarray(twist),
        jnp.asarray(pick),
        jnp.asarray(lag_table()),
    )

def settle_kernel(from_ref, to_ref, held, sems):
    count = 4
    parts = [pl.ds(k * (HALF // count), HALF // count) for k in range(count)]
    into = [pltpu.make_async_copy(from_ref.at[p], held.at[p], sems.at[0, k])
            for k, p in enumerate(parts)]
    onto = [pltpu.make_async_copy(held.at[p], to_ref.at[p], sems.at[1, k])
            for k, p in enumerate(parts)]
    for copy in into:
        copy.start()
    for one, two in zip(into, onto):
        one.wait()
        two.start()
    for copy in onto:
        copy.wait()


def shards(records, limits, sources):
    result = correlations(records, limits, sources)
    hbm = pl.BlockSpec(memory_space=pl.ANY)
    return pl.pallas_call(
        settle_kernel,
        out_shape=jax.ShapeDtypeStruct(result.shape, result.dtype),
        in_specs=[hbm],
        out_specs=hbm,
        scratch_shapes=[
            pltpu.VMEM(result.shape, result.dtype), pltpu.SemaphoreType.DMA((2, 4))
        ],
        compiler_params=pltpu.CompilerParams(vmem_limit_bytes=57 << 20),
        name="settle",
    )(result)


def solution(mesh):
    in_specs = (P(None, "chan", None), P(), P())
    out_specs = P("segment", "chan", None)
    return jax.shard_map(shards, mesh=mesh, in_specs=in_specs, out_specs=out_specs, check_vma=False)
```

```python
import functools
import math

import jax
import jax.numpy as jnp
import numpy as np
from jax import lax
from jax.experimental import pallas as pl
from jax.experimental.pallas import tpu as pltpu
from jax.sharding import PartitionSpec as P

NCH = 10240
NT = 7680
NF = 512
FLO = 32
NVS = 256
STRIDE = 10
LAGS = 512
MB = 4

epsilon = 1e-06

SEG = 2
NY, NX, NZ = 4, 4, 8
CHIPS = NY * NX * NZ
CH_DEV = NCH // CHIPS
F_DEV = NF // CHIPS
M_DEV = MB // SEG
SEQS = F_DEV * M_DEV
RECS = CH_DEV // STRIDE
VBLOCK = 32
HALF = NVS // SEG
LANES = 128
HALF_SEQS = SEQS // 2
WIDE = HALF_SEQS * CH_DEV
PLANE = NY * NX
RADIX = 4
STEPS = 5
QUARTER = NT // RADIX
KBLOCK = QUARTER // STEPS
ROWS = M_DEV * CH_DEV
MESH = pl.DeviceIdType.MESH
FAR_Z = sorted(range(1, NZ), key=lambda d: -min(d, NZ - d))
FAR_PLANE = sorted(
    range(1, NY * NX), key=lambda d: -min(d // NX, NY - d // NX) - min(d % NX, NX - d % NX)
)
BF = jnp.bfloat16
F32 = jnp.float32


def as_bf16(array):
    return np.asarray(array, np.float32).astype(jnp.bfloat16)


def split(array):
    high = as_bf16(array)
    low = as_bf16(np.asarray(array, np.float64) - high.astype(np.float64))
    return high, low


def time_tables():
    plane, late = np.meshgrid(np.arange(PLANE), np.arange(NZ // RADIX))
    chips = plane * NZ + RADIX * late
    bins = FLO + CHIPS * np.arange(F_DEV)[:, None] + chips.reshape(1, -1)
    times = np.arange(QUARTER, dtype=np.int64)
    tables = []
    for residue in range(RADIX):
        freqs = (bins + residue).reshape(-1)
        phase = times[:, None] * freqs[None, :] % NT
        angle = phase.astype(np.float32) * np.float32(2.0 * math.pi / NT)
        tables.append(np.concatenate([np.cos(angle), -np.sin(angle)], axis=1))
    table = np.stack(tables).reshape(RADIX, STEPS, KBLOCK, 2 * CHIPS)
    return as_bf16(table.transpose(1, 0, 2, 3))


def lag_table():
    lagged = np.arange(LAGS, dtype=np.int64) - LAGS // 2
    freqs = FLO + np.arange(NF, dtype=np.int64)
    phase = freqs[:, None] * lagged[None, :] % NT
    angle = phase.astype(np.float32) * np.float32(2.0 * math.pi / NT)
    return as_bf16(np.stack([np.cos(angle), -np.sin(angle)]).reshape(2, 2, NF // 2, LAGS)
                   .transpose(1, 0, 2, 3).reshape(2, NF, LAGS))


def roots(rows, cols, modulus):
    phase = np.arange(rows)[:, None] * np.arange(cols)[None, :] % modulus
    angle = phase * (2.0 * math.pi / modulus)
    return np.cos(angle), -np.sin(angle)


def filter_tables():
    dr, di = roots(CHIPS, CHIPS, CHIPS)
    er = np.zeros((LANES, LANES))
    ei = np.zeros((LANES, LANES))
    er[:CH_DEV, :CH_DEV], ei[:CH_DEV, :CH_DEV] = roots(CH_DEV, CH_DEV, CH_DEV)
    tr = np.zeros((CHIPS, LANES))
    ti = np.zeros((CHIPS, LANES))
    tr[:, :CH_DEV], ti[:, :CH_DEV] = roots(CHIPS, CH_DEV, NCH)
    outer = np.block([[dr, -di], [di, dr]])
    inner = np.block([[er, ei], [-ei, er]])
    inner_back = np.block([[er, -ei], [ei, er]])
    outer_back = np.block([[dr, di], [-di, dr]])
    major = np.arange(CHIPS).reshape(PLANE, NZ).T.reshape(-1)
    outer_z = np.block([[dr[:, major], -di[:, major]], [di[:, major], dr[:, major]]])
    order = (outer, inner, inner_back, outer_back, outer_z)
    tables = np.stack([t for m in order for t in split(m)])
    twist = np.stack([tr, ti]).astype(np.float32)
    pick = np.zeros((2, HALF_SEQS, LANES, LANES), np.float32)
    for part in range(2):
        for q in range(HALF_SEQS):
            for u in range(RECS):
                pick[part, q, STRIDE * u, (q * 2 + part) * RECS + u] = 1.0
    return tables, twist, as_bf16(pick.reshape(2, HALF_SEQS * LANES, LANES))


def mm(left, right):
    return jnp.dot(left, right, preferred_element_type=F32)


def mm_nt(left, right):
    return lax.dot_general(left, right, (((1,), (1,)), ((), ())), preferred_element_type=F32)


def halves(value):
    high = value.astype(BF)
    return high, (value - high.astype(F32)).astype(BF)


def filter_half(h, x, column, limit_ref, tables, twist):
    tail = jnp.zeros((CHIPS, LANES // 2), BF)
    xs = jnp.concatenate(
        [
            jnp.concatenate([x[:, :WIDE], tail], axis=1),
            jnp.concatenate([x[:, WIDE:], tail], axis=1),
        ],
        axis=0,
    )
    outer = 0 if h == 0 else 8
    first = mm(tables[outer], xs) + mm(tables[outer + 1], xs)
    tr, ti = twist[0], twist[1]
    turned = []
    for q in range(HALF_SEQS):
        yr = first[:CHIPS, CH_DEV * q : CH_DEV * q + LANES]
        yi = first[CHIPS:, CH_DEV * q : CH_DEV * q + LANES]
        turned.append(jnp.concatenate([yr * tr - yi * ti, yr * ti + yi * tr], axis=1))
    high, low = halves(jnp.concatenate(turned, axis=0))
    wave = mm(high, tables[2]) + mm(high, tables[3]) + mm(low, tables[2])
    shape = (CHIPS, 2 * LANES)
    lane = lax.broadcasted_iota(jnp.int32, shape, 1) % LANES
    index = lax.broadcasted_iota(jnp.int32, shape, 0) + CHIPS * lane
    signed = jnp.where(index < NCH // 2, index, index - NCH)
    reach = jnp.where(index < NCH, jnp.abs(signed), NCH)
    kept = []
    for q in range(HALF_SEQS):
        limit = limit_ref[0, (2 * h + q // M_DEV) * CHIPS + column]
        kept.append(jnp.where(reach <= limit, wave[CHIPS * q : CHIPS * (q + 1)], 0.0))
    high, low = halves(jnp.concatenate(kept, axis=0))
    back = mm(high, tables[4]) + mm(high, tables[5]) + mm(low, tables[4])
    real, imag = [], []
    for q in range(HALF_SEQS):
        ur = back[CHIPS * q : CHIPS * (q + 1), :LANES]
        ui = back[CHIPS * q : CHIPS * (q + 1), LANES:]
        real.append(ur * tr + ui * ti)
        imag.append(ui * tr - ur * ti)
    high, low = halves(
        jnp.concatenate([jnp.concatenate(real, axis=1), jnp.concatenate(imag, axis=1)], axis=0)
    )
    field = mm(tables[6], high) + mm(tables[6], low) + mm(tables[7], high)
    return (field * (1.0 / NCH)).astype(BF)


def hot_sources(source):
    chip = ((source.astype(F32) + 0.5) * (1.0 / CH_DEV)).astype(jnp.int32)
    inside = source - CH_DEV * chip
    rows = lax.broadcasted_iota(jnp.int32, (LANES, NVS), 0)
    hot_inside = jnp.where(rows == inside, 1.0, 0.0).astype(BF)
    hot_chip = jnp.where(rows == chip, 1.0, 0.0)
    return hot_inside, hot_chip


def source_rows(field, hot_inside, hot_chip):
    lines = []
    for q in range(HALF_SEQS):
        for part in range(2):
            block = field[CHIPS * part : CHIPS * (part + 1), LANES * q : LANES * (q + 1)]
            chosen = mm(block, hot_inside) * hot_chip
            lines.append(jnp.sum(chosen, axis=0, keepdims=True))
    return jnp.concatenate(lines, axis=0).astype(BF)


def reorder(new, old):
    rows = lax.broadcasted_iota(jnp.int32, (CHIPS, CHIPS), 0)
    cols = lax.broadcasted_iota(jnp.int32, (CHIPS, CHIPS), 1)
    return jnp.where(cols == old(*new(rows)), 1.0, 0.0).astype(BF)


def sources_across(h, s_all, flat, st, eye):
    lines = 2 * HALF_SEQS
    for g in range(SEG):
        flat[...] = s_all[h, g].reshape(CHIPS * lines, HALF).astype(F32)
        for n in range(lines):
            st[g, n] = mm_nt(eye, flat[pl.ds(n, CHIPS, stride=lines), :].astype(BF))


def correlate_half(h, st, rt, lag, cross, total, keep):
    blocks = HALF // VBLOCK

    def spread_block(b):
        for f in range(F_DEV // 2):
            rr, ri = [], []
            for g in range(SEG):
                for m in range(M_DEV):
                    at = ((f * M_DEV + m) * 2) * RECS
                    rr.append(rt[g, at : at + RECS])
                    ri.append(rt[g, at + RECS : at + 2 * RECS])
            for v in range(VBLOCK // 8):
                rows = slice(b * VBLOCK + v * 8, b * VBLOCK + v * 8 + 8)
                cr = jnp.zeros((8, RECS, LANES), F32)
                ci = jnp.zeros((8, RECS, LANES), F32)
                for g in range(SEG):
                    for m in range(M_DEV):
                        n = (f * M_DEV + m) * 2
                        sr = st[g, n, rows, :][:, None, :]
                        si = st[g, n + 1, rows, :][:, None, :]
                        r, i = rr[g * M_DEV + m][None], ri[g * M_DEV + m][None]
                        cr = cr + sr * r + si * i
                        ci = ci + sr * i - si * r
                to = slice(v * 8 * RECS, (v + 1) * 8 * RECS)
                cross[b, to, f * LANES : (f + 1) * LANES] = cr.reshape(8 * RECS, LANES).astype(BF)
                cross[b, to, NF // 2 + f * LANES : NF // 2 + (f + 1) * LANES] = (
                    ci.reshape(8 * RECS, LANES).astype(BF)
                )

    def lag_block(b):
        result = mm(cross[b], lag[h])
        if h == 0:
            total[b] = result
        else:
            keep(b, (result + total[b]) * (1.0 / math.sqrt(MB * NF)))

    for b in range(blocks):
        spread_block(b)
        if b:
            lag_block(b - 1)
    lag_block(blocks - 1)


def whole_kernel(records, time_ref, limit_hbm, src_hbm, tables_hbm, twist_hbm, pick_hbm,
                    lag_hbm, out_ref, s_all, r_fin, flat, st, rt, cross, total, lag,
                    limit_ref, src_ref, result_buf,
                    xbuf, tbuf, acc, tables, twist, pick,
                    a, g0, b0, x0, b1, g1, b2, x1, s_in, r_in, ry, rx,
                    in_sem, late_sem, come, gone, pass_sem):
    seg = lax.axis_index("segment")
    chan = lax.axis_index("chan")
    z = lax.rem(chan, NZ)
    plane = lax.div(chan, NZ)
    x = lax.rem(plane, NX)
    y = lax.div(plane, NX)

    def zpeer(d, ds=0):
        return (lax.rem(seg + ds, SEG), plane * NZ + lax.rem(z + d, NZ))

    def ppeer(d):
        return (seg, lax.rem(plane + d, PLANE) * NZ + z)

    def xpeer(d):
        return (seg, (y * NX + lax.rem(x + d, NX)) * NZ + z)

    def ypeer(d):
        return (seg, (lax.rem(y + d, NY) * NX + x) * NZ + z)

    def remote(src, dst, send, recv, device):
        copy = pltpu.make_async_remote_copy(
            src_ref=src, dst_ref=dst, send_sem=send, recv_sem=recv,
            device_id=device, device_id_type=MESH,
        )
        copy.start()
        return copy

    def local(src, dst, sem):
        copy = pltpu.make_async_copy(src, dst, sem)
        copy.start()
        return copy

    def settled(ref, sem):
        pltpu.make_async_copy(ref, ref, sem).wait()

    def fetch(k):
        span = slice(k * KBLOCK, (k + 1) * KBLOCK)
        for s in range(RADIX):
            local(records.at[pl.ds(M_DEV * seg, M_DEV), :, pl.ds(QUARTER * s + KBLOCK * k, KBLOCK)],
                  xbuf.at[s, :, :, span], in_sem.at[0, k])
        local(time_ref.at[k], tbuf.at[k], in_sem.at[1, k])

    fetch(0)
    fetch(1)

    peers = [zpeer(d, ds) for ds in range(SEG) for d in range(NZ) if d or ds]
    peers += [ppeer(d) for d in range(1, PLANE)]
    barrier = pltpu.get_barrier_semaphore()
    for peer in peers:
        pl.semaphore_signal(barrier, inc=1, device_id=peer, device_id_type=MESH)
    for k in range(2, STEPS):
        fetch(k)
    later = [local(tables_hbm, tables, late_sem.at[0]), local(twist_hbm, twist, late_sem.at[1]),
             local(pick_hbm, pick, late_sem.at[2]), local(limit_hbm, limit_ref, late_sem.at[3]),
             local(src_hbm, src_ref, late_sem.at[4])]
    lag_load = local(lag_hbm, lag, late_sem.at[5])

    for k in range(STEPS):
        settled(xbuf.at[:, :, :, k * KBLOCK : (k + 1) * KBLOCK], in_sem.at[0, k])
        settled(tbuf.at[k], in_sem.at[1, k])
        q0, q1, q2, q3 = [
            xbuf[s, :, :, k * KBLOCK : (k + 1) * KBLOCK].reshape(ROWS, KBLOCK).astype(F32)
            for s in range(RADIX)
        ]
        s02, s13, d02, d13 = q0 + q2, q1 + q3, (q0 - q2).astype(BF), (q1 - q3).astype(BF)
        whole, rest = halves(s02 + s13)
        turn = (s02 - s13).astype(BF)
        sums = (
            mm(whole, tbuf[k, 0]) + mm(rest, tbuf[k, 0]),
            mm(turn, tbuf[k, 2]),
            mm(d02, tbuf[k, 1]),
            mm(d13, tbuf[k, 1]),
            mm(d02, tbuf[k, 3]),
            mm(d13, tbuf[k, 3]),
        )
        for n in range(6):
            if k == 0:
                acc[n] = sums[n]
            else:
                acc[n] += sums[n]

    def turned_by(n, sign):
        real = acc[n, :, :CHIPS] + sign * acc[n + 1, :, CHIPS:]
        imag = acc[n, :, CHIPS:] - sign * acc[n + 1, :, :CHIPS]
        return jnp.concatenate([real, imag], axis=1)

    scale = 1.0 / math.sqrt(NT)
    spectra = [v * scale for v in (acc[0], turned_by(2, 1.0), acc[1], turned_by(4, -1.0))]
    squares = sum(v * v for v in spectra)
    power = jnp.sum(squares, axis=1, keepdims=True) * (1.0 / NF)
    factor = lax.rsqrt(power + epsilon)
    rows = lax.broadcasted_iota(jnp.int32, (2 * CHIPS, 2 * CHIPS), 0)
    cols = lax.broadcasted_iota(jnp.int32, (2 * CHIPS, 2 * CHIPS), 1)
    eye = jnp.where(rows == cols, 1.0, 0.0).astype(BF)
    white = [mm_nt(eye, (v * factor).astype(BF)) for v in spectra]
    group = CHIPS // RADIX

    def assemble(h):
        for r in range(RADIX):
            blocks = []
            for part_of in range(2):
                for f in (2 * h, 2 * h + 1):
                    at = part_of * CHIPS + f * group
                    blocks.append(white[r][at : at + group])
            joined = jnp.concatenate(blocks, axis=1).astype(BF)
            a[h, 2 * r : 2 * r + 2] = joined.reshape(2, PLANE, 2 * WIDE)

    def slot(t):
        return lax.rem(t, RADIX) * 2 + lax.div(t, RADIX)

    assemble(0)
    pl.semaphore_wait(barrier, len(peers))
    def cross_z(source, target, n, index):
        for d in FAR_Z:
            remote(source.at[index(lax.rem(z + d, NZ))], target.at[z], gone.at[n], come.at[n], zpeer(d))
        local(source.at[index(z)], target.at[z], come.at[n])

    def cross_plane(source, target, n):
        for d in FAR_PLANE:
            remote(source.at[lax.rem(plane + d, PLANE)], target.at[plane], gone.at[n], come.at[n],
                   ppeer(d))
        local(source.at[plane], target.at[plane], come.at[n])

    cross_z(a.at[0], g0, 0, slot)
    assemble(1)
    to_plane = reorder(lambda r: (r % NZ, r // NZ),
                       lambda t, p: ((t % RADIX) * 2 + t // RADIX) * PLANE + p)
    b1[...] = mm(to_plane, a[1].reshape(CHIPS, 2 * WIDE)).astype(BF).reshape(PLANE, NZ, 2 * WIDE)
    cross_plane(b1, g1, 1)
    from_z = reorder(lambda r: (r % NZ, r // NZ), lambda t, p: t * PLANE + p)
    to_z = reorder(lambda r: (r % PLANE, r // PLANE), lambda p, t: p * NZ + t)
    settled(g0, come.at[0])
    b0[...] = mm(from_z, g0[...].reshape(CHIPS, 2 * WIDE)).astype(BF).reshape(PLANE, NZ, 2 * WIDE)
    cross_plane(b0, x0, 2)
    settled(g1, come.at[1])
    b2[...] = mm(to_z, g1[...].reshape(CHIPS, 2 * WIDE)).astype(BF).reshape(NZ, PLANE, 2 * WIDE)
    cross_z(b2, x1, 3, lambda t: t)
    for copy in later:
        copy.wait()
    hot_inside, hot_chip = hot_sources(src_ref[...])
    settled(x0, come.at[2])
    field = filter_half(0, x0[...].reshape(CHIPS, 2 * WIDE), chan, limit_ref, tables, twist)
    found = source_rows(field, hot_inside, hot_chip)
    s_in[0, 0] = found[:, :HALF]
    s_in[0, 1] = found[:, HALF:]

    def send_z(h):
        for d in FAR_Z + [0]:
            for ds in range(SEG):
                if d or ds:
                    remote(s_in.at[h, lax.rem(seg + ds, SEG)], s_all.at[h, seg, y, x, z],
                           gone.at[4 + h], come.at[4 + h], zpeer(d, ds))
        local(s_in.at[h, seg], s_all.at[h, seg, y, x, z], come.at[4 + h])

    def sent_z(h):
        settled(b1.at[pl.ds(0, 3)], gone.at[4 + h])

    first_axis, second_axis = (xpeer, ypeer), (ypeer, xpeer)

    def block(h, p, d, e):
        if p == 0:
            return s_all.at[h, 0, lax.rem(y + e, NY), lax.rem(x + NX - d, NX)]
        return s_all.at[h, 1, lax.rem(y + NY - d, NY), lax.rem(x + e, NX)]

    def send_block(h, p, d, e, kind, device):
        one = block(h, p, d, e)
        early = (kind == 1 and d % 2 == 0) or (kind == 2 and d % 2 == 1)
        recv = pass_sem.at[1, h, p, d] if early else come.at[6 + h]
        return remote(one, one, gone.at[(8 if kind == 3 else 6) + h], recv, device)

    def phase_own(h):
        along = [None] * 4
        for d in (2, 1, 3):
            along[d] = [remote(block(h, p, 0, 0), block(h, p, 0, 0), gone.at[10 + h],
                               pass_sem.at[0, h, p, d], first_axis[p](d)) for p in range(2)]
        up = [None] * 4
        down = [None] * 4
        up[0] = [send_block(h, p, 0, 0, 1, second_axis[p](1)) for p in range(2)]
        down[0] = [send_block(h, p, 0, 0, 2, second_axis[p](3)) for p in range(2)]
        return along, up, down

    def phase_across(h, along, up, down):
        for d in (1, 3, 2):
            up[d], down[d] = [], []
            for p in range(2):
                along[d][p].wait_recv()
                up[d].append(send_block(h, p, d, 0, 1, second_axis[p](1)))
                down[d].append(send_block(h, p, d, 0, 2, second_axis[p](3)))

    def phase_relay(h, up, down):
        for d in (0, 1, 3, 2):
            for p in range(2):
                if d % 2 == 0:
                    up[d][p].wait_recv()
                    send_block(h, p, d, 3, 3, second_axis[p](1))
                else:
                    down[d][p].wait_recv()
                    send_block(h, p, d, 1, 3, second_axis[p](3))

    def phase_done(h):
        settled(s_all.at[h, 0], come.at[6 + h])

    def phase_sent(h):
        settled(s_all.at[h, 0], gone.at[6 + h])
        settled(s_all.at[h, 0, pl.ds(0, 2)], gone.at[8 + h])
        settled(s_all.at[h, :, pl.ds(0, 3), 0], gone.at[10 + h])

    def receivers(h, field):
        found = mm(field[:CHIPS], pick[0]) + mm(field[CHIPS:], pick[1])
        r_in[h] = found.reshape(NY, NX, NZ, 1, LANES)

    def r_send_y(h):
        for d in (2, 1, 3):
            remote(r_in.at[h, lax.rem(y + d, NY)], ry.at[h, y], gone.at[12 + h], come.at[8 + h], ypeer(d))
        local(r_in.at[h, y], ry.at[h, y], come.at[8 + h])

    def r_send_x(h):
        settled(ry.at[h], come.at[8 + h])
        for d in (2, 1, 3):
            remote(ry.at[h, :, lax.rem(x + d, NX)], rx.at[h, :, x], gone.at[14 + h], come.at[10 + h],
                   xpeer(d))
        local(ry.at[h, :, x], rx.at[h, :, x], come.at[10 + h])

    def r_send_z(h):
        settled(rx.at[h], come.at[10 + h])
        for d in FAR_Z + [0]:
            for ds in range(SEG):
                if d or ds:
                    remote(rx.at[h, :, :, lax.rem(z + d, NZ)], r_fin.at[h, seg, :, :, z],
                           gone.at[16 + h], come.at[12 + h], zpeer(d, ds))
        local(rx.at[h, :, :, z], r_fin.at[h, seg, :, :, z], come.at[12 + h])

    def r_sent(h):
        settled(r_in.at[h, pl.ds(0, 3)], gone.at[12 + h])
        settled(ry.at[h, :, pl.ds(0, 3)], gone.at[14 + h])

    def receivers_across(h):
        for g in range(SEG):
            rt[g] = mm_nt(small, r_fin[h, g].reshape(CHIPS, LANES).astype(BF))

    small = eye[:LANES, :LANES]
    send_z(0)
    receivers(0, field)
    r_send_y(0)
    settled(x1, come.at[3])
    field = filter_half(1, x1[...].reshape(CHIPS, 2 * WIDE), chan, limit_ref, tables, twist)
    found = source_rows(field, hot_inside, hot_chip)
    s_in[1, 0] = found[:, :HALF]
    s_in[1, 1] = found[:, HALF:]
    send_z(1)
    receivers(1, field)
    r_send_y(1)
    r_send_x(0)
    settled(s_all.at[0, 0, 0, pl.ds(0, 2)], come.at[4])
    along0, up0, down0 = phase_own(0)
    settled(a.at[0, pl.ds(0, NZ - 1)], gone.at[0])
    settled(b1.at[pl.ds(0, PLANE - 1)], gone.at[1])
    settled(b0.at[pl.ds(0, PLANE - 1)], gone.at[2])
    settled(b2.at[pl.ds(0, NZ - 1)], gone.at[3])
    r_send_x(1)
    r_send_z(0)
    phase_across(0, along0, up0, down0)
    settled(s_all.at[1, 0, 0, pl.ds(0, 2)], come.at[5])
    along1, up1, down1 = phase_own(1)
    r_send_z(1)
    phase_relay(0, up0, down0)
    sent_z(0)
    sent_z(1)
    r_sent(0)
    r_sent(1)
    phase_across(1, along1, up1, down1)
    phase_done(0)
    sources_across(0, s_all, flat, st, small)
    phase_relay(1, up1, down1)
    settled(r_fin.at[0], come.at[12])
    receivers_across(0)
    lag_load.wait()
    correlate_half(0, st, rt, lag, cross, total, None)
    settled(b1.at[pl.ds(0, 12)], gone.at[16])
    settled(b1.at[pl.ds(0, 12)], gone.at[17])
    phase_sent(0)
    settled(r_fin.at[1], come.at[13])
    receivers_across(1)
    phase_done(1)
    sources_across(1, s_all, flat, st, small)

    def keep(b, result):
        part = slice(b * VBLOCK, (b + 1) * VBLOCK)
        result_buf[part] = result.astype(BF).reshape(VBLOCK, RECS, LAGS)
        at = pl.ds(b * VBLOCK, VBLOCK)
        local(result_buf.at[at], out_ref.at[at], late_sem.at[6])

    correlate_half(1, st, rt, lag, cross, total, keep)
    phase_sent(1)
    settled(result_buf, late_sem.at[6])


def correlations(records, limits, sources):
    tables, twist, pick = filter_tables()
    hbm = pl.BlockSpec(memory_space=pl.ANY)
    dma = pltpu.SemaphoreType.DMA
    by_z = pltpu.VMEM((NZ, PLANE, 2 * WIDE), BF)
    by_plane = pltpu.VMEM((PLANE, NZ, 2 * WIDE), BF)
    grid_of = pltpu.VMEM((2, NY, NX, NZ, 1, LANES), F32)
    return pl.pallas_call(
        whole_kernel,
        out_shape=jax.ShapeDtypeStruct((HALF, RECS, LAGS), BF),
        in_specs=[hbm] * 8,
        out_specs=hbm,
        scratch_shapes=[
            pltpu.VMEM((2, SEG, NY, NX, NZ, SEQS, HALF), BF),
            pltpu.VMEM((2, SEG, NY, NX, NZ, 1, LANES), F32),
            pltpu.VMEM((CHIPS * SEQS, HALF), F32),
            pltpu.VMEM((SEG, SEQS, HALF, CHIPS), F32),
            pltpu.VMEM((SEG, LANES, CHIPS), F32),
            pltpu.VMEM((HALF // VBLOCK, VBLOCK * RECS, NF), BF),
            pltpu.VMEM((HALF // VBLOCK, VBLOCK * RECS, LAGS), F32),
            pltpu.VMEM((2, NF, LAGS), BF),
            pltpu.SMEM((1, NF), jnp.int32),
            pltpu.VMEM((1, NVS), jnp.int32),
            pltpu.VMEM((HALF, RECS, LAGS), BF),
            pltpu.VMEM((RADIX, M_DEV, CH_DEV, QUARTER), BF),
            pltpu.VMEM((STEPS, RADIX, KBLOCK, 2 * CHIPS), BF),
            pltpu.VMEM((6, ROWS, 2 * CHIPS), F32),
            pltpu.VMEM(tables.shape, BF),
            pltpu.VMEM(twist.shape, F32),
            pltpu.VMEM(pick.shape, BF),
            pltpu.VMEM((2, NZ, PLANE, 2 * WIDE), BF),
            by_z, by_plane, by_plane, by_plane, by_plane, by_z, by_z,
            pltpu.VMEM((2, SEG, SEQS, HALF), BF),
            grid_of, grid_of, grid_of,
            dma((2, STEPS)), dma((7,)), dma((14,)), dma((18,)), dma((2, 2, 2, NX)),
        ],
        compiler_params=pltpu.CompilerParams(
            collective_id=0, has_side_effects=True, vmem_limit_bytes=57 << 20
        ),
        cost_estimate=pl.CostEstimate(flops=6 << 30, bytes_accessed=12 << 20, transcendentals=0),
        name="correlations",
    )(
        records,
        jnp.asarray(time_tables()),
        limits.reshape(1, NF),
        sources.reshape(1, NVS),
        jnp.asarray(tables),
        jnp.asarray(twist),
        jnp.asarray(pick),
        jnp.asarray(lag_table()),
    )

def settle_kernel(from_ref, to_ref, held, sems):
    count = 4
    parts = [pl.ds(k * (HALF // count), HALF // count) for k in range(count)]
    into = [pltpu.make_async_copy(from_ref.at[p], held.at[p], sems.at[0, k])
            for k, p in enumerate(parts)]
    onto = [pltpu.make_async_copy(held.at[p], to_ref.at[p], sems.at[1, k])
            for k, p in enumerate(parts)]
    for copy in into:
        copy.start()
    for one, two in zip(into, onto):
        one.wait()
        two.start()
    for copy in onto:
        copy.wait()


def shards(records, limits, sources):
    result = correlations(records, limits, sources)
    hbm = pl.BlockSpec(memory_space=pl.ANY)
    return pl.pallas_call(
        settle_kernel,
        out_shape=jax.ShapeDtypeStruct(result.shape, result.dtype),
        in_specs=[hbm],
        out_specs=hbm,
        scratch_shapes=[
            pltpu.VMEM(result.shape, result.dtype), pltpu.SemaphoreType.DMA((2, 4))
        ],
        compiler_params=pltpu.CompilerParams(vmem_limit_bytes=57 << 20),
        name="settle",
    )(result)


def solution(mesh):
    in_specs = (P(None, "chan", None), P(), P())
    out_specs = P("segment", "chan", None)
    return jax.shard_map(shards, mesh=mesh, in_specs=in_specs, out_specs=out_specs, check_vma=False)
```

```python
import functools
import math

import jax
import jax.numpy as jnp
import numpy as np
from jax import lax
from jax.experimental import pallas as pl
from jax.experimental.pallas import tpu as pltpu
from jax.sharding import PartitionSpec as P

NCH = 10240
NT = 7680
NF = 512
FLO = 32
NVS = 256
STRIDE = 10
LAGS = 512
MB = 4

epsilon = 1e-06

SEG = 2
NY, NX, NZ = 4, 4, 8
CHIPS = NY * NX * NZ
CH_DEV = NCH // CHIPS
F_DEV = NF // CHIPS
M_DEV = MB // SEG
SEQS = F_DEV * M_DEV
RECS = CH_DEV // STRIDE
VBLOCK = 32
HALF = NVS // SEG
LANES = 128
HALF_SEQS = SEQS // 2
WIDE = HALF_SEQS * CH_DEV
PLANE = NY * NX
RADIX = 4
STEPS = 5
QUARTER = NT // RADIX
KBLOCK = QUARTER // STEPS
ROWS = M_DEV * CH_DEV
MESH = pl.DeviceIdType.MESH
FAR_Z = sorted(range(1, NZ), key=lambda d: -min(d, NZ - d))
FAR_PLANE = sorted(
    range(1, NY * NX), key=lambda d: -min(d // NX, NY - d // NX) - min(d % NX, NX - d % NX)
)
BF = jnp.bfloat16
F32 = jnp.float32


def as_bf16(array):
    return np.asarray(array, np.float32).astype(jnp.bfloat16)


def split(array):
    high = as_bf16(array)
    low = as_bf16(np.asarray(array, np.float64) - high.astype(np.float64))
    return high, low


def time_tables():
    plane, late = np.meshgrid(np.arange(PLANE), np.arange(NZ // RADIX))
    chips = plane * NZ + RADIX * late
    bins = FLO + CHIPS * np.arange(F_DEV)[:, None] + chips.reshape(1, -1)
    times = np.arange(QUARTER, dtype=np.int64)
    tables = []
    for residue in range(RADIX):
        freqs = (bins + residue).reshape(-1)
        phase = times[:, None] * freqs[None, :] % NT
        angle = phase.astype(np.float32) * np.float32(2.0 * math.pi / NT)
        tables.append(np.concatenate([np.cos(angle), -np.sin(angle)], axis=1))
    table = np.stack(tables).reshape(RADIX, STEPS, KBLOCK, 2 * CHIPS)
    return as_bf16(table.transpose(1, 0, 2, 3))


def lag_table():
    lagged = np.arange(LAGS, dtype=np.int64) - LAGS // 2
    freqs = FLO + np.arange(NF, dtype=np.int64)
    phase = freqs[:, None] * lagged[None, :] % NT
    angle = phase.astype(np.float32) * np.float32(2.0 * math.pi / NT)
    return as_bf16(np.stack([np.cos(angle), -np.sin(angle)]).reshape(2, 2, NF // 2, LAGS)
                   .transpose(1, 0, 2, 3).reshape(2, NF, LAGS))


def roots(rows, cols, modulus):
    phase = np.arange(rows)[:, None] * np.arange(cols)[None, :] % modulus
    angle = phase * (2.0 * math.pi / modulus)
    return np.cos(angle), -np.sin(angle)


def filter_tables():
    dr, di = roots(CHIPS, CHIPS, CHIPS)
    er = np.zeros((LANES, LANES))
    ei = np.zeros((LANES, LANES))
    er[:CH_DEV, :CH_DEV], ei[:CH_DEV, :CH_DEV] = roots(CH_DEV, CH_DEV, CH_DEV)
    tr = np.zeros((CHIPS, LANES))
    ti = np.zeros((CHIPS, LANES))
    tr[:, :CH_DEV], ti[:, :CH_DEV] = roots(CHIPS, CH_DEV, NCH)
    outer = np.block([[dr, -di], [di, dr]])
    inner = np.block([[er, ei], [-ei, er]])
    inner_back = np.block([[er, -ei], [ei, er]])
    outer_back = np.block([[dr, di], [-di, dr]])
    major = np.arange(CHIPS).reshape(PLANE, NZ).T.reshape(-1)
    outer_z = np.block([[dr[:, major], -di[:, major]], [di[:, major], dr[:, major]]])
    order = (outer, inner, inner_back, outer_back, outer_z)
    tables = np.stack([t for m in order for t in split(m)])
    twist = np.stack([tr, ti]).astype(np.float32)
    pick = np.zeros((2, HALF_SEQS, LANES, LANES), np.float32)
    for part in range(2):
        for q in range(HALF_SEQS):
            for u in range(RECS):
                pick[part, q, STRIDE * u, (q * 2 + part) * RECS + u] = 1.0
    return tables, twist, as_bf16(pick.reshape(2, HALF_SEQS * LANES, LANES))


def mm(left, right):
    return jnp.dot(left, right, preferred_element_type=F32)


def mm_nt(left, right):
    return lax.dot_general(left, right, (((1,), (1,)), ((), ())), preferred_element_type=F32)


def halves(value):
    high = value.astype(BF)
    return high, (value - high.astype(F32)).astype(BF)


def filter_half(h, x, column, limit_ref, tables, twist):
    tail = jnp.zeros((CHIPS, LANES // 2), BF)
    xs = jnp.concatenate(
        [
            jnp.concatenate([x[:, :WIDE], tail], axis=1),
            jnp.concatenate([x[:, WIDE:], tail], axis=1),
        ],
        axis=0,
    )
    outer = 0 if h == 0 else 8
    first = mm(tables[outer], xs) + mm(tables[outer + 1], xs)
    tr, ti = twist[0], twist[1]
    turned = []
    for q in range(HALF_SEQS):
        yr = first[:CHIPS, CH_DEV * q : CH_DEV * q + LANES]
        yi = first[CHIPS:, CH_DEV * q : CH_DEV * q + LANES]
        turned.append(jnp.concatenate([yr * tr - yi * ti, yr * ti + yi * tr], axis=1))
    high, low = halves(jnp.concatenate(turned, axis=0))
    wave = mm(high, tables[2]) + mm(high, tables[3]) + mm(low, tables[2])
    shape = (CHIPS, 2 * LANES)
    lane = lax.broadcasted_iota(jnp.int32, shape, 1) % LANES
    index = lax.broadcasted_iota(jnp.int32, shape, 0) + CHIPS * lane
    signed = jnp.where(index < NCH // 2, index, index - NCH)
    reach = jnp.where(index < NCH, jnp.abs(signed), NCH)
    kept = []
    for q in range(HALF_SEQS):
        limit = limit_ref[0, (2 * h + q // M_DEV) * CHIPS + column]
        kept.append(jnp.where(reach <= limit, wave[CHIPS * q : CHIPS * (q + 1)], 0.0))
    high, low = halves(jnp.concatenate(kept, axis=0))
    back = mm(high, tables[4]) + mm(high, tables[5]) + mm(low, tables[4])
    real, imag = [], []
    for q in range(HALF_SEQS):
        ur = back[CHIPS * q : CHIPS * (q + 1), :LANES]
        ui = back[CHIPS * q : CHIPS * (q + 1), LANES:]
        real.append(ur * tr + ui * ti)
        imag.append(ui * tr - ur * ti)
    high, low = halves(
        jnp.concatenate([jnp.concatenate(real, axis=1), jnp.concatenate(imag, axis=1)], axis=0)
    )
    field = mm(tables[6], high) + mm(tables[6], low) + mm(tables[7], high)
    return (field * (1.0 / NCH)).astype(BF)


def hot_sources(source):
    chip = ((source.astype(F32) + 0.5) * (1.0 / CH_DEV)).astype(jnp.int32)
    inside = source - CH_DEV * chip
    rows = lax.broadcasted_iota(jnp.int32, (LANES, NVS), 0)
    hot_inside = jnp.where(rows == inside, 1.0, 0.0).astype(BF)
    hot_chip = jnp.where(rows == chip, 1.0, 0.0)
    return hot_inside, hot_chip


def source_rows(field, hot_inside, hot_chip):
    lines = []
    for q in range(HALF_SEQS):
        for part in range(2):
            block = field[CHIPS * part : CHIPS * (part + 1), LANES * q : LANES * (q + 1)]
            chosen = mm(block, hot_inside) * hot_chip
            lines.append(jnp.sum(chosen, axis=0, keepdims=True))
    return jnp.concatenate(lines, axis=0).astype(BF)


def reorder(new, old):
    rows = lax.broadcasted_iota(jnp.int32, (CHIPS, CHIPS), 0)
    cols = lax.broadcasted_iota(jnp.int32, (CHIPS, CHIPS), 1)
    return jnp.where(cols == old(*new(rows)), 1.0, 0.0).astype(BF)


def sources_across(h, s_all, flat, st, eye):
    lines = 2 * HALF_SEQS
    for g in range(SEG):
        flat[...] = s_all[h, g].reshape(CHIPS * lines, HALF).astype(F32)
        for n in range(lines):
            st[g, n] = mm_nt(eye, flat[pl.ds(n, CHIPS, stride=lines), :].astype(BF))


def correlate_half(h, st, rt, lag, cross, total, keep):
    blocks = HALF // VBLOCK

    def spread_block(b):
        for f in range(F_DEV // 2):
            rr, ri = [], []
            for g in range(SEG):
                for m in range(M_DEV):
                    at = ((f * M_DEV + m) * 2) * RECS
                    rr.append(rt[g, at : at + RECS])
                    ri.append(rt[g, at + RECS : at + 2 * RECS])
            for v in range(VBLOCK // 8):
                crs, cis = [], []
                for w in range(8):
                    row = b * VBLOCK + v * 8 + w
                    cr = ci = None
                    for g in range(SEG):
                        for m in range(M_DEV):
                            n = (f * M_DEV + m) * 2
                            sr = st[g, n, row : row + 1, :]
                            si = st[g, n + 1, row : row + 1, :]
                            r, i = rr[g * M_DEV + m], ri[g * M_DEV + m]
                            one, two = sr * r + si * i, sr * i - si * r
                            cr = one if cr is None else cr + one
                            ci = two if ci is None else ci + two
                    crs.append(cr)
                    cis.append(ci)
                cr = jnp.concatenate(crs, axis=0)
                ci = jnp.concatenate(cis, axis=0)
                to = slice(v * 8 * RECS, (v + 1) * 8 * RECS)
                cross[b, to, f * LANES : (f + 1) * LANES] = cr.reshape(8 * RECS, LANES).astype(BF)
                cross[b, to, NF // 2 + f * LANES : NF // 2 + (f + 1) * LANES] = (
                    ci.reshape(8 * RECS, LANES).astype(BF)
                )

    def lag_block(b):
        result = mm(cross[b], lag[h])
        if h == 0:
            total[b] = result
        else:
            keep(b, (result + total[b]) * (1.0 / math.sqrt(MB * NF)))

    for b in range(blocks):
        spread_block(b)
        if b:
            lag_block(b - 1)
    lag_block(blocks - 1)


def whole_kernel(records, time_ref, limit_hbm, src_hbm, tables_hbm, twist_hbm, pick_hbm,
                    lag_hbm, out_ref, s_all, r_fin, flat, st, rt, cross, total, lag,
                    limit_ref, src_ref, result_buf,
                    xbuf, tbuf, acc, tables, twist, pick,
                    a, g0, b0, x0, b1, g1, b2, x1, s_in, r_in, ry, rx,
                    in_sem, late_sem, come, gone, pass_sem):
    seg = lax.axis_index("segment")
    chan = lax.axis_index("chan")
    z = lax.rem(chan, NZ)
    plane = lax.div(chan, NZ)
    x = lax.rem(plane, NX)
    y = lax.div(plane, NX)

    def zpeer(d, ds=0):
        return (lax.rem(seg + ds, SEG), plane * NZ + lax.rem(z + d, NZ))

    def ppeer(d):
        return (seg, lax.rem(plane + d, PLANE) * NZ + z)

    def xpeer(d):
        return (seg, (y * NX + lax.rem(x + d, NX)) * NZ + z)

    def ypeer(d):
        return (seg, (lax.rem(y + d, NY) * NX + x) * NZ + z)

    def remote(src, dst, send, recv, device):
        copy = pltpu.make_async_remote_copy(
            src_ref=src, dst_ref=dst, send_sem=send, recv_sem=recv,
            device_id=device, device_id_type=MESH,
        )
        copy.start()
        return copy

    def local(src, dst, sem):
        copy = pltpu.make_async_copy(src, dst, sem)
        copy.start()
        return copy

    def settled(ref, sem):
        pltpu.make_async_copy(ref, ref, sem).wait()

    def fetch(k):
        span = slice(k * KBLOCK, (k + 1) * KBLOCK)
        for s in range(RADIX):
            local(records.at[pl.ds(M_DEV * seg, M_DEV), :, pl.ds(QUARTER * s + KBLOCK * k, KBLOCK)],
                  xbuf.at[s, :, :, span], in_sem.at[0, k])
        local(time_ref.at[k], tbuf.at[k], in_sem.at[1, k])

    fetch(0)
    fetch(1)

    peers = [zpeer(d, ds) for ds in range(SEG) for d in range(NZ) if d or ds]
    peers += [ppeer(d) for d in range(1, PLANE)]
    barrier = pltpu.get_barrier_semaphore()
    for peer in peers:
        pl.semaphore_signal(barrier, inc=1, device_id=peer, device_id_type=MESH)
    for k in range(2, STEPS):
        fetch(k)
    later = [local(tables_hbm, tables, late_sem.at[0]), local(twist_hbm, twist, late_sem.at[1]),
             local(pick_hbm, pick, late_sem.at[2]), local(limit_hbm, limit_ref, late_sem.at[3]),
             local(src_hbm, src_ref, late_sem.at[4])]
    lag_load = local(lag_hbm, lag, late_sem.at[5])

    for k in range(STEPS):
        settled(xbuf.at[:, :, :, k * KBLOCK : (k + 1) * KBLOCK], in_sem.at[0, k])
        settled(tbuf.at[k], in_sem.at[1, k])
        q0, q1, q2, q3 = [
            xbuf[s, :, :, k * KBLOCK : (k + 1) * KBLOCK].reshape(ROWS, KBLOCK).astype(F32)
            for s in range(RADIX)
        ]
        s02, s13, d02, d13 = q0 + q2, q1 + q3, (q0 - q2).astype(BF), (q1 - q3).astype(BF)
        whole, rest = halves(s02 + s13)
        turn = (s02 - s13).astype(BF)
        sums = (
            mm(whole, tbuf[k, 0]) + mm(rest, tbuf[k, 0]),
            mm(turn, tbuf[k, 2]),
            mm(d02, tbuf[k, 1]),
            mm(d13, tbuf[k, 1]),
            mm(d02, tbuf[k, 3]),
            mm(d13, tbuf[k, 3]),
        )
        for n in range(6):
            if k == 0:
                acc[n] = sums[n]
            else:
                acc[n] += sums[n]

    def turned_by(n, sign):
        real = acc[n, :, :CHIPS] + sign * acc[n + 1, :, CHIPS:]
        imag = acc[n, :, CHIPS:] - sign * acc[n + 1, :, :CHIPS]
        return jnp.concatenate([real, imag], axis=1)

    scale = 1.0 / math.sqrt(NT)
    spectra = [v * scale for v in (acc[0], turned_by(2, 1.0), acc[1], turned_by(4, -1.0))]
    squares = sum(v * v for v in spectra)
    power = jnp.sum(squares, axis=1, keepdims=True) * (1.0 / NF)
    factor = lax.rsqrt(power + epsilon)
    rows = lax.broadcasted_iota(jnp.int32, (2 * CHIPS, 2 * CHIPS), 0)
    cols = lax.broadcasted_iota(jnp.int32, (2 * CHIPS, 2 * CHIPS), 1)
    eye = jnp.where(rows == cols, 1.0, 0.0).astype(BF)
    white = [mm_nt(eye, (v * factor).astype(BF)) for v in spectra]
    group = CHIPS // RADIX

    def assemble(h):
        for r in range(RADIX):
            blocks = []
            for part_of in range(2):
                for f in (2 * h, 2 * h + 1):
                    at = part_of * CHIPS + f * group
                    blocks.append(white[r][at : at + group])
            joined = jnp.concatenate(blocks, axis=1).astype(BF)
            a[h, 2 * r : 2 * r + 2] = joined.reshape(2, PLANE, 2 * WIDE)

    def slot(t):
        return lax.rem(t, RADIX) * 2 + lax.div(t, RADIX)

    assemble(0)
    pl.semaphore_wait(barrier, len(peers))
    def cross_z(source, target, n, index):
        for d in FAR_Z:
            remote(source.at[index(lax.rem(z + d, NZ))], target.at[z], gone.at[n], come.at[n], zpeer(d))
        local(source.at[index(z)], target.at[z], come.at[n])

    def cross_plane(source, target, n):
        for d in FAR_PLANE:
            remote(source.at[lax.rem(plane + d, PLANE)], target.at[plane], gone.at[n], come.at[n],
                   ppeer(d))
        local(source.at[plane], target.at[plane], come.at[n])

    cross_z(a.at[0], g0, 0, slot)
    assemble(1)
    to_plane = reorder(lambda r: (r % NZ, r // NZ),
                       lambda t, p: ((t % RADIX) * 2 + t // RADIX) * PLANE + p)
    b1[...] = mm(to_plane, a[1].reshape(CHIPS, 2 * WIDE)).astype(BF).reshape(PLANE, NZ, 2 * WIDE)
    cross_plane(b1, g1, 1)
    from_z = reorder(lambda r: (r % NZ, r // NZ), lambda t, p: t * PLANE + p)
    to_z = reorder(lambda r: (r % PLANE, r // PLANE), lambda p, t: p * NZ + t)
    settled(g0, come.at[0])
    b0[...] = mm(from_z, g0[...].reshape(CHIPS, 2 * WIDE)).astype(BF).reshape(PLANE, NZ, 2 * WIDE)
    cross_plane(b0, x0, 2)
    settled(g1, come.at[1])
    b2[...] = mm(to_z, g1[...].reshape(CHIPS, 2 * WIDE)).astype(BF).reshape(NZ, PLANE, 2 * WIDE)
    cross_z(b2, x1, 3, lambda t: t)
    for copy in later:
        copy.wait()
    hot_inside, hot_chip = hot_sources(src_ref[...])
    settled(x0, come.at[2])
    field = filter_half(0, x0[...].reshape(CHIPS, 2 * WIDE), chan, limit_ref, tables, twist)
    found = source_rows(field, hot_inside, hot_chip)
    s_in[0, 0] = found[:, :HALF]
    s_in[0, 1] = found[:, HALF:]

    def send_z(h):
        for d in FAR_Z + [0]:
            for ds in range(SEG):
                if d or ds:
                    remote(s_in.at[h, lax.rem(seg + ds, SEG)], s_all.at[h, seg, y, x, z],
                           gone.at[4 + h], come.at[4 + h], zpeer(d, ds))
        local(s_in.at[h, seg], s_all.at[h, seg, y, x, z], come.at[4 + h])

    def sent_z(h):
        settled(b1.at[pl.ds(0, 3)], gone.at[4 + h])

    first_axis, second_axis = (xpeer, ypeer), (ypeer, xpeer)

    def block(h, p, d, e):
        if p == 0:
            return s_all.at[h, 0, lax.rem(y + e, NY), lax.rem(x + NX - d, NX)]
        return s_all.at[h, 1, lax.rem(y + NY - d, NY), lax.rem(x + e, NX)]

    def send_block(h, p, d, e, kind, device):
        one = block(h, p, d, e)
        early = (kind == 1 and d % 2 == 0) or (kind == 2 and d % 2 == 1)
        recv = pass_sem.at[1, h, p, d] if early else come.at[6 + h]
        return remote(one, one, gone.at[(8 if kind == 3 else 6) + h], recv, device)

    def phase_own(h):
        along = [None] * 4
        for d in (2, 1, 3):
            along[d] = [remote(block(h, p, 0, 0), block(h, p, 0, 0), gone.at[10 + h],
                               pass_sem.at[0, h, p, d], first_axis[p](d)) for p in range(2)]
        up = [None] * 4
        down = [None] * 4
        up[0] = [send_block(h, p, 0, 0, 1, second_axis[p](1)) for p in range(2)]
        down[0] = [send_block(h, p, 0, 0, 2, second_axis[p](3)) for p in range(2)]
        return along, up, down

    def phase_across(h, along, up, down):
        for d in (1, 3, 2):
            up[d], down[d] = [], []
            for p in range(2):
                along[d][p].wait_recv()
                up[d].append(send_block(h, p, d, 0, 1, second_axis[p](1)))
                down[d].append(send_block(h, p, d, 0, 2, second_axis[p](3)))

    def phase_relay(h, up, down):
        for d in (0, 1, 3, 2):
            for p in range(2):
                if d % 2 == 0:
                    up[d][p].wait_recv()
                    send_block(h, p, d, 3, 3, second_axis[p](1))
                else:
                    down[d][p].wait_recv()
                    send_block(h, p, d, 1, 3, second_axis[p](3))

    def phase_done(h):
        settled(s_all.at[h, 0], come.at[6 + h])

    def phase_sent(h):
        settled(s_all.at[h, 0], gone.at[6 + h])
        settled(s_all.at[h, 0, pl.ds(0, 2)], gone.at[8 + h])
        settled(s_all.at[h, :, pl.ds(0, 3), 0], gone.at[10 + h])

    def receivers(h, field):
        found = mm(field[:CHIPS], pick[0]) + mm(field[CHIPS:], pick[1])
        r_in[h] = found.reshape(NY, NX, NZ, 1, LANES)

    def r_send_y(h):
        for d in (2, 1, 3):
            remote(r_in.at[h, lax.rem(y + d, NY)], ry.at[h, y], gone.at[12 + h], come.at[8 + h], ypeer(d))
        local(r_in.at[h, y], ry.at[h, y], come.at[8 + h])

    def r_send_x(h):
        settled(ry.at[h], come.at[8 + h])
        for d in (2, 1, 3):
            remote(ry.at[h, :, lax.rem(x + d, NX)], rx.at[h, :, x], gone.at[14 + h], come.at[10 + h],
                   xpeer(d))
        local(ry.at[h, :, x], rx.at[h, :, x], come.at[10 + h])

    def r_send_z(h):
        settled(rx.at[h], come.at[10 + h])
        for d in FAR_Z + [0]:
            for ds in range(SEG):
                if d or ds:
                    remote(rx.at[h, :, :, lax.rem(z + d, NZ)], r_fin.at[h, seg, :, :, z],
                           gone.at[16 + h], come.at[12 + h], zpeer(d, ds))
        local(rx.at[h, :, :, z], r_fin.at[h, seg, :, :, z], come.at[12 + h])

    def r_sent(h):
        settled(r_in.at[h, pl.ds(0, 3)], gone.at[12 + h])
        settled(ry.at[h, :, pl.ds(0, 3)], gone.at[14 + h])

    def receivers_across(h):
        for g in range(SEG):
            rt[g] = mm_nt(small, r_fin[h, g].reshape(CHIPS, LANES).astype(BF))

    small = eye[:LANES, :LANES]
    send_z(0)
    receivers(0, field)
    r_send_y(0)
    settled(x1, come.at[3])
    field = filter_half(1, x1[...].reshape(CHIPS, 2 * WIDE), chan, limit_ref, tables, twist)
    found = source_rows(field, hot_inside, hot_chip)
    s_in[1, 0] = found[:, :HALF]
    s_in[1, 1] = found[:, HALF:]
    send_z(1)
    receivers(1, field)
    r_send_y(1)
    r_send_x(0)
    settled(s_all.at[0, 0, 0, pl.ds(0, 2)], come.at[4])
    along0, up0, down0 = phase_own(0)
    settled(a.at[0, pl.ds(0, NZ - 1)], gone.at[0])
    settled(b1.at[pl.ds(0, PLANE - 1)], gone.at[1])
    settled(b0.at[pl.ds(0, PLANE - 1)], gone.at[2])
    settled(b2.at[pl.ds(0, NZ - 1)], gone.at[3])
    r_send_x(1)
    r_send_z(0)
    phase_across(0, along0, up0, down0)
    settled(s_all.at[1, 0, 0, pl.ds(0, 2)], come.at[5])
    along1, up1, down1 = phase_own(1)
    r_send_z(1)
    phase_relay(0, up0, down0)
    sent_z(0)
    sent_z(1)
    r_sent(0)
    r_sent(1)
    phase_across(1, along1, up1, down1)
    phase_done(0)
    sources_across(0, s_all, flat, st, small)
    phase_relay(1, up1, down1)
    settled(r_fin.at[0], come.at[12])
    receivers_across(0)
    lag_load.wait()
    correlate_half(0, st, rt, lag, cross, total, None)
    settled(b1.at[pl.ds(0, 12)], gone.at[16])
    settled(b1.at[pl.ds(0, 12)], gone.at[17])
    phase_sent(0)
    settled(r_fin.at[1], come.at[13])
    receivers_across(1)
    phase_done(1)
    sources_across(1, s_all, flat, st, small)

    def keep(b, result):
        part = slice(b * VBLOCK, (b + 1) * VBLOCK)
        result_buf[part] = result.astype(BF).reshape(VBLOCK, RECS, LAGS)
        at = pl.ds(b * VBLOCK, VBLOCK)
        local(result_buf.at[at], out_ref.at[at], late_sem.at[6])

    correlate_half(1, st, rt, lag, cross, total, keep)
    phase_sent(1)
    settled(result_buf, late_sem.at[6])


def correlations(records, limits, sources):
    tables, twist, pick = filter_tables()
    hbm = pl.BlockSpec(memory_space=pl.ANY)
    dma = pltpu.SemaphoreType.DMA
    by_z = pltpu.VMEM((NZ, PLANE, 2 * WIDE), BF)
    by_plane = pltpu.VMEM((PLANE, NZ, 2 * WIDE), BF)
    grid_of = pltpu.VMEM((2, NY, NX, NZ, 1, LANES), F32)
    return pl.pallas_call(
        whole_kernel,
        out_shape=jax.ShapeDtypeStruct((HALF, RECS, LAGS), BF),
        in_specs=[hbm] * 8,
        out_specs=hbm,
        scratch_shapes=[
            pltpu.VMEM((2, SEG, NY, NX, NZ, SEQS, HALF), BF),
            pltpu.VMEM((2, SEG, NY, NX, NZ, 1, LANES), F32),
            pltpu.VMEM((CHIPS * SEQS, HALF), F32),
            pltpu.VMEM((SEG, SEQS, HALF, CHIPS), F32),
            pltpu.VMEM((SEG, LANES, CHIPS), F32),
            pltpu.VMEM((HALF // VBLOCK, VBLOCK * RECS, NF), BF),
            pltpu.VMEM((HALF // VBLOCK, VBLOCK * RECS, LAGS), F32),
            pltpu.VMEM((2, NF, LAGS), BF),
            pltpu.SMEM((1, NF), jnp.int32),
            pltpu.VMEM((1, NVS), jnp.int32),
            pltpu.VMEM((HALF, RECS, LAGS), BF),
            pltpu.VMEM((RADIX, M_DEV, CH_DEV, QUARTER), BF),
            pltpu.VMEM((STEPS, RADIX, KBLOCK, 2 * CHIPS), BF),
            pltpu.VMEM((6, ROWS, 2 * CHIPS), F32),
            pltpu.VMEM(tables.shape, BF),
            pltpu.VMEM(twist.shape, F32),
            pltpu.VMEM(pick.shape, BF),
            pltpu.VMEM((2, NZ, PLANE, 2 * WIDE), BF),
            by_z, by_plane, by_plane, by_plane, by_plane, by_z, by_z,
            pltpu.VMEM((2, SEG, SEQS, HALF), BF),
            grid_of, grid_of, grid_of,
            dma((2, STEPS)), dma((7,)), dma((14,)), dma((18,)), dma((2, 2, 2, NX)),
        ],
        compiler_params=pltpu.CompilerParams(
            collective_id=0, has_side_effects=True, vmem_limit_bytes=57 << 20
        ),
        cost_estimate=pl.CostEstimate(flops=6 << 30, bytes_accessed=12 << 20, transcendentals=0),
        name="correlations",
    )(
        records,
        jnp.asarray(time_tables()),
        limits.reshape(1, NF),
        sources.reshape(1, NVS),
        jnp.asarray(tables),
        jnp.asarray(twist),
        jnp.asarray(pick),
        jnp.asarray(lag_table()),
    )

def settle_kernel(from_ref, to_ref, held, sems):
    count = 4
    parts = [pl.ds(k * (HALF // count), HALF // count) for k in range(count)]
    into = [pltpu.make_async_copy(from_ref.at[p], held.at[p], sems.at[0, k])
            for k, p in enumerate(parts)]
    onto = [pltpu.make_async_copy(held.at[p], to_ref.at[p], sems.at[1, k])
            for k, p in enumerate(parts)]
    for copy in into:
        copy.start()
    for one, two in zip(into, onto):
        one.wait()
        two.start()
    for copy in onto:
        copy.wait()


def shards(records, limits, sources):
    result = correlations(records, limits, sources)
    hbm = pl.BlockSpec(memory_space=pl.ANY)
    return pl.pallas_call(
        settle_kernel,
        out_shape=jax.ShapeDtypeStruct(result.shape, result.dtype),
        in_specs=[hbm],
        out_specs=hbm,
        scratch_shapes=[
            pltpu.VMEM(result.shape, result.dtype), pltpu.SemaphoreType.DMA((2, 4))
        ],
        compiler_params=pltpu.CompilerParams(vmem_limit_bytes=57 << 20),
        name="settle",
    )(result)


def solution(mesh):
    in_specs = (P(None, "chan", None), P(), P())
    out_specs = P("segment", "chan", None)
    return jax.shard_map(shards, mesh=mesh, in_specs=in_specs, out_specs=out_specs, check_vma=False)
```

```python
import functools
import math

import jax
import jax.numpy as jnp
import numpy as np
from jax import lax
from jax.experimental import pallas as pl
from jax.experimental.pallas import tpu as pltpu
from jax.sharding import PartitionSpec as P

NCH = 10240
NT = 7680
NF = 512
FLO = 32
NVS = 256
STRIDE = 10
LAGS = 512
MB = 4

epsilon = 1e-06

SEG = 2
NY, NX, NZ = 4, 4, 8
CHIPS = NY * NX * NZ
CH_DEV = NCH // CHIPS
F_DEV = NF // CHIPS
M_DEV = MB // SEG
SEQS = F_DEV * M_DEV
RECS = CH_DEV // STRIDE
VBLOCK = 32
HALF = NVS // SEG
LANES = 128
HALF_SEQS = SEQS // 2
WIDE = HALF_SEQS * CH_DEV
PLANE = NY * NX
RADIX = 4
STEPS = 5
QUARTER = NT // RADIX
KBLOCK = QUARTER // STEPS
ROWS = M_DEV * CH_DEV
MESH = pl.DeviceIdType.MESH
FAR_Z = sorted(range(1, NZ), key=lambda d: -min(d, NZ - d))
FAR_PLANE = sorted(
    range(1, NY * NX), key=lambda d: -min(d // NX, NY - d // NX) - min(d % NX, NX - d % NX)
)
BF = jnp.bfloat16
F32 = jnp.float32


def as_bf16(array):
    return np.asarray(array, np.float32).astype(jnp.bfloat16)


def split(array):
    high = as_bf16(array)
    low = as_bf16(np.asarray(array, np.float64) - high.astype(np.float64))
    return high, low


def time_tables():
    plane, late = np.meshgrid(np.arange(PLANE), np.arange(NZ // RADIX))
    chips = plane * NZ + RADIX * late
    bins = FLO + CHIPS * np.arange(F_DEV)[:, None] + chips.reshape(1, -1)
    times = np.arange(QUARTER, dtype=np.int64)
    tables = []
    for residue in range(RADIX):
        freqs = (bins + residue).reshape(-1)
        phase = times[:, None] * freqs[None, :] % NT
        angle = phase.astype(np.float32) * np.float32(2.0 * math.pi / NT)
        tables.append(np.concatenate([np.cos(angle), -np.sin(angle)], axis=1))
    table = np.stack(tables).reshape(RADIX, STEPS, KBLOCK, 2 * CHIPS)
    return as_bf16(table.transpose(1, 0, 2, 3))


def lag_table():
    lagged = np.arange(LAGS, dtype=np.int64) - LAGS // 2
    freqs = FLO + np.arange(NF, dtype=np.int64)
    phase = freqs[:, None] * lagged[None, :] % NT
    angle = phase.astype(np.float32) * np.float32(2.0 * math.pi / NT)
    return as_bf16(np.stack([np.cos(angle), -np.sin(angle)]).reshape(2, 2, NF // 2, LAGS)
                   .transpose(1, 0, 2, 3).reshape(2, NF, LAGS))


def roots(rows, cols, modulus):
    phase = np.arange(rows)[:, None] * np.arange(cols)[None, :] % modulus
    angle = phase * (2.0 * math.pi / modulus)
    return np.cos(angle), -np.sin(angle)


def filter_tables():
    dr, di = roots(CHIPS, CHIPS, CHIPS)
    er = np.zeros((LANES, LANES))
    ei = np.zeros((LANES, LANES))
    er[:CH_DEV, :CH_DEV], ei[:CH_DEV, :CH_DEV] = roots(CH_DEV, CH_DEV, CH_DEV)
    tr = np.zeros((CHIPS, LANES))
    ti = np.zeros((CHIPS, LANES))
    tr[:, :CH_DEV], ti[:, :CH_DEV] = roots(CHIPS, CH_DEV, NCH)
    outer = np.block([[dr, -di], [di, dr]])
    inner = np.block([[er, ei], [-ei, er]])
    inner_back = np.block([[er, -ei], [ei, er]])
    outer_back = np.block([[dr, di], [-di, dr]])
    major = np.arange(CHIPS).reshape(PLANE, NZ).T.reshape(-1)
    outer_z = np.block([[dr[:, major], -di[:, major]], [di[:, major], dr[:, major]]])
    order = (outer, inner, inner_back, outer_back, outer_z)
    tables = np.stack([t for m in order for t in split(m)])
    twist = np.stack([tr, ti]).astype(np.float32)
    pick = np.zeros((2, HALF_SEQS, LANES, LANES), np.float32)
    for part in range(2):
        for q in range(HALF_SEQS):
            for u in range(RECS):
                pick[part, q, STRIDE * u, (q * 2 + part) * RECS + u] = 1.0
    return tables, twist, as_bf16(pick.reshape(2, HALF_SEQS * LANES, LANES))


def mm(left, right):
    return jnp.dot(left, right, preferred_element_type=F32)


def mm_nt(left, right):
    return lax.dot_general(left, right, (((1,), (1,)), ((), ())), preferred_element_type=F32)


def halves(value):
    high = value.astype(BF)
    return high, (value - high.astype(F32)).astype(BF)


def filter_half(h, x, column, limit_ref, tables, twist):
    tail = jnp.zeros((CHIPS, LANES // 2), BF)
    xs = jnp.concatenate(
        [
            jnp.concatenate([x[:, :WIDE], tail], axis=1),
            jnp.concatenate([x[:, WIDE:], tail], axis=1),
        ],
        axis=0,
    )
    outer = 0 if h == 0 else 8
    first = mm(tables[outer], xs) + mm(tables[outer + 1], xs)
    tr, ti = twist[0], twist[1]
    turned = []
    for q in range(HALF_SEQS):
        yr = first[:CHIPS, CH_DEV * q : CH_DEV * q + LANES]
        yi = first[CHIPS:, CH_DEV * q : CH_DEV * q + LANES]
        turned.append(jnp.concatenate([yr * tr - yi * ti, yr * ti + yi * tr], axis=1))
    high, low = halves(jnp.concatenate(turned, axis=0))
    wave = mm(high, tables[2]) + mm(high, tables[3]) + mm(low, tables[2])
    shape = (CHIPS, 2 * LANES)
    lane = lax.broadcasted_iota(jnp.int32, shape, 1) % LANES
    index = lax.broadcasted_iota(jnp.int32, shape, 0) + CHIPS * lane
    signed = jnp.where(index < NCH // 2, index, index - NCH)
    reach = jnp.where(index < NCH, jnp.abs(signed), NCH)
    kept = []
    for q in range(HALF_SEQS):
        limit = limit_ref[0, (2 * h + q // M_DEV) * CHIPS + column]
        kept.append(jnp.where(reach <= limit, wave[CHIPS * q : CHIPS * (q + 1)], 0.0))
    high, low = halves(jnp.concatenate(kept, axis=0))
    back = mm(high, tables[4]) + mm(high, tables[5]) + mm(low, tables[4])
    real, imag = [], []
    for q in range(HALF_SEQS):
        ur = back[CHIPS * q : CHIPS * (q + 1), :LANES]
        ui = back[CHIPS * q : CHIPS * (q + 1), LANES:]
        real.append(ur * tr + ui * ti)
        imag.append(ui * tr - ur * ti)
    high, low = halves(
        jnp.concatenate([jnp.concatenate(real, axis=1), jnp.concatenate(imag, axis=1)], axis=0)
    )
    field = mm(tables[6], high) + mm(tables[6], low) + mm(tables[7], high)
    return (field * (1.0 / NCH)).astype(BF)


def hot_sources(source):
    chip = ((source.astype(F32) + 0.5) * (1.0 / CH_DEV)).astype(jnp.int32)
    inside = source - CH_DEV * chip
    rows = lax.broadcasted_iota(jnp.int32, (LANES, NVS), 0)
    hot_inside = jnp.where(rows == inside, 1.0, 0.0).astype(BF)
    hot_chip = jnp.where(rows == chip, 1.0, 0.0)
    return hot_inside, hot_chip


def source_rows(field, hot_inside, hot_chip):
    lines = []
    for q in range(HALF_SEQS):
        for part in range(2):
            block = field[CHIPS * part : CHIPS * (part + 1), LANES * q : LANES * (q + 1)]
            chosen = mm(block, hot_inside) * hot_chip
            lines.append(jnp.sum(chosen, axis=0, keepdims=True))
    return jnp.concatenate(lines, axis=0).astype(BF)


def reorder(new, old):
    rows = lax.broadcasted_iota(jnp.int32, (CHIPS, CHIPS), 0)
    cols = lax.broadcasted_iota(jnp.int32, (CHIPS, CHIPS), 1)
    return jnp.where(cols == old(*new(rows)), 1.0, 0.0).astype(BF)


def sources_across(h, s_all, flat, st, eye):
    lines = 2 * HALF_SEQS
    for g in range(SEG):
        flat[...] = s_all[h, g].reshape(CHIPS * lines, HALF).astype(F32)
        for n in range(lines):
            st[g, n] = mm_nt(eye, flat[pl.ds(n, CHIPS, stride=lines), :].astype(BF))


def correlate_half(h, st, rt, lag, cross, total, keep):
    blocks = HALF // VBLOCK

    def spread_block(b):
        for f in range(F_DEV // 2):
            rr, ri = [], []
            for g in range(SEG):
                for m in range(M_DEV):
                    at = ((f * M_DEV + m) * 2) * RECS
                    rr.append(rt[g, at : at + RECS])
                    ri.append(rt[g, at + RECS : at + 2 * RECS])
            for v in range(VBLOCK // 8):
                crs, cis = [], []
                for w in range(8):
                    row = b * VBLOCK + v * 8 + w
                    cr = ci = None
                    for g in range(SEG):
                        for m in range(M_DEV):
                            n = (f * M_DEV + m) * 2
                            sr = st[g, n, row : row + 1, :]
                            si = st[g, n + 1, row : row + 1, :]
                            r, i = rr[g * M_DEV + m], ri[g * M_DEV + m]
                            one, two = sr * r + si * i, sr * i - si * r
                            cr = one if cr is None else cr + one
                            ci = two if ci is None else ci + two
                    crs.append(cr)
                    cis.append(ci)
                cr = jnp.concatenate(crs, axis=0)
                ci = jnp.concatenate(cis, axis=0)
                to = slice(v * 8 * RECS, (v + 1) * 8 * RECS)
                cross[b, to, f * LANES : (f + 1) * LANES] = cr.reshape(8 * RECS, LANES).astype(BF)
                cross[b, to, NF // 2 + f * LANES : NF // 2 + (f + 1) * LANES] = (
                    ci.reshape(8 * RECS, LANES).astype(BF)
                )

    def lag_block(b):
        result = mm(cross[b], lag[h])
        if h == 0:
            total[b] = result
        else:
            keep(b, (result + total[b]) * (1.0 / math.sqrt(MB * NF)))

    for b in range(blocks):
        spread_block(b)
        if b:
            lag_block(b - 1)
    lag_block(blocks - 1)


def whole_kernel(records, time_ref, limit_hbm, src_hbm, tables_hbm, twist_hbm, pick_hbm,
                    lag_hbm, out_ref, s_all, r_fin, flat, st, rt, cross, total, lag,
                    limit_ref, src_ref, result_buf,
                    xbuf, tbuf, acc, tables, twist, pick,
                    a, g0, b0, x0, b1, g1, b2, x1, s_in, r_in, ry, rx,
                    in_sem, late_sem, come, gone, pass_sem):
    seg = lax.axis_index("segment")
    chan = lax.axis_index("chan")
    z = lax.rem(chan, NZ)
    plane = lax.div(chan, NZ)
    x = lax.rem(plane, NX)
    y = lax.div(plane, NX)

    def zpeer(d, ds=0):
        return (lax.rem(seg + ds, SEG), plane * NZ + lax.rem(z + d, NZ))

    def ppeer(d):
        return (seg, lax.rem(plane + d, PLANE) * NZ + z)

    def xpeer(d):
        return (seg, (y * NX + lax.rem(x + d, NX)) * NZ + z)

    def ypeer(d):
        return (seg, (lax.rem(y + d, NY) * NX + x) * NZ + z)

    def remote(src, dst, send, recv, device):
        copy = pltpu.make_async_remote_copy(
            src_ref=src, dst_ref=dst, send_sem=send, recv_sem=recv,
            device_id=device, device_id_type=MESH,
        )
        copy.start()
        return copy

    def local(src, dst, sem):
        copy = pltpu.make_async_copy(src, dst, sem)
        copy.start()
        return copy

    def settled(ref, sem):
        pltpu.make_async_copy(ref, ref, sem).wait()

    def fetch(k):
        span = slice(k * KBLOCK, (k + 1) * KBLOCK)
        for s in range(RADIX):
            local(records.at[pl.ds(M_DEV * seg, M_DEV), :, pl.ds(QUARTER * s + KBLOCK * k, KBLOCK)],
                  xbuf.at[s, :, :, span], in_sem.at[0, k])
        local(time_ref.at[k], tbuf.at[k], in_sem.at[1, k])

    fetch(0)
    fetch(1)

    peers = [zpeer(d, ds) for ds in range(SEG) for d in range(NZ) if d or ds]
    peers += [ppeer(d) for d in range(1, PLANE)]
    barrier = pltpu.get_barrier_semaphore()
    for peer in peers:
        pl.semaphore_signal(barrier, inc=1, device_id=peer, device_id_type=MESH)
    for k in range(2, STEPS):
        fetch(k)
    later = [local(tables_hbm, tables, late_sem.at[0]), local(twist_hbm, twist, late_sem.at[1]),
             local(pick_hbm, pick, late_sem.at[2]), local(limit_hbm, limit_ref, late_sem.at[3]),
             local(src_hbm, src_ref, late_sem.at[4])]
    lag_load = local(lag_hbm, lag, late_sem.at[5])

    for k in range(STEPS):
        settled(xbuf.at[:, :, :, k * KBLOCK : (k + 1) * KBLOCK], in_sem.at[0, k])
        settled(tbuf.at[k], in_sem.at[1, k])
        q0, q1, q2, q3 = [
            xbuf[s, :, :, k * KBLOCK : (k + 1) * KBLOCK].reshape(ROWS, KBLOCK).astype(F32)
            for s in range(RADIX)
        ]
        s02, s13, d02, d13 = q0 + q2, q1 + q3, (q0 - q2).astype(BF), (q1 - q3).astype(BF)
        whole, rest = halves(s02 + s13)
        turn = (s02 - s13).astype(BF)
        sums = (
            mm(whole, tbuf[k, 0]) + mm(rest, tbuf[k, 0]),
            mm(turn, tbuf[k, 2]),
            mm(d02, tbuf[k, 1]),
            mm(d13, tbuf[k, 1]),
            mm(d02, tbuf[k, 3]),
            mm(d13, tbuf[k, 3]),
        )
        for n in range(6):
            if k == 0:
                acc[n] = sums[n]
            else:
                acc[n] += sums[n]

    def turned_by(n, sign):
        real = acc[n, :, :CHIPS] + sign * acc[n + 1, :, CHIPS:]
        imag = acc[n, :, CHIPS:] - sign * acc[n + 1, :, :CHIPS]
        return jnp.concatenate([real, imag], axis=1)

    scale = 1.0 / math.sqrt(NT)
    spectra = [v * scale for v in (acc[0], turned_by(2, 1.0), acc[1], turned_by(4, -1.0))]
    squares = sum(v * v for v in spectra)
    power = jnp.sum(squares, axis=1, keepdims=True) * (1.0 / NF)
    factor = lax.rsqrt(power + epsilon)
    rows = lax.broadcasted_iota(jnp.int32, (2 * CHIPS, 2 * CHIPS), 0)
    cols = lax.broadcasted_iota(jnp.int32, (2 * CHIPS, 2 * CHIPS), 1)
    eye = jnp.where(rows == cols, 1.0, 0.0).astype(BF)
    white = [mm_nt(eye, (v * factor).astype(BF)) for v in spectra]
    group = CHIPS // RADIX

    def assemble(h):
        for r in range(RADIX):
            blocks = []
            for part_of in range(2):
                for f in (2 * h, 2 * h + 1):
                    at = part_of * CHIPS + f * group
                    blocks.append(white[r][at : at + group])
            joined = jnp.concatenate(blocks, axis=1).astype(BF)
            a[h, 2 * r : 2 * r + 2] = joined.reshape(2, PLANE, 2 * WIDE)

    def slot(t):
        return lax.rem(t, RADIX) * 2 + lax.div(t, RADIX)

    assemble(0)
    pl.semaphore_wait(barrier, len(peers))
    def cross_z(source, target, n, index):
        for d in FAR_Z:
            remote(source.at[index(lax.rem(z + d, NZ))], target.at[z], gone.at[n], come.at[n], zpeer(d))
        local(source.at[index(z)], target.at[z], come.at[n])

    def cross_plane(source, target, n):
        for d in FAR_PLANE:
            remote(source.at[lax.rem(plane + d, PLANE)], target.at[plane], gone.at[n], come.at[n],
                   ppeer(d))
        local(source.at[plane], target.at[plane], come.at[n])

    cross_z(a.at[0], g0, 0, slot)
    assemble(1)
    to_plane = reorder(lambda r: (r % NZ, r // NZ),
                       lambda t, p: ((t % RADIX) * 2 + t // RADIX) * PLANE + p)
    b1[...] = mm(to_plane, a[1].reshape(CHIPS, 2 * WIDE)).astype(BF).reshape(PLANE, NZ, 2 * WIDE)
    cross_plane(b1, g1, 1)
    from_z = reorder(lambda r: (r % NZ, r // NZ), lambda t, p: t * PLANE + p)
    to_z = reorder(lambda r: (r % PLANE, r // PLANE), lambda p, t: p * NZ + t)
    settled(g0, come.at[0])
    b0[...] = mm(from_z, g0[...].reshape(CHIPS, 2 * WIDE)).astype(BF).reshape(PLANE, NZ, 2 * WIDE)
    cross_plane(b0, x0, 2)
    settled(g1, come.at[1])
    b2[...] = mm(to_z, g1[...].reshape(CHIPS, 2 * WIDE)).astype(BF).reshape(NZ, PLANE, 2 * WIDE)
    cross_z(b2, x1, 3, lambda t: t)
    for copy in later:
        copy.wait()
    hot_inside, hot_chip = hot_sources(src_ref[...])
    settled(x0, come.at[2])
    field = filter_half(0, x0[...].reshape(CHIPS, 2 * WIDE), chan, limit_ref, tables, twist)
    found = source_rows(field, hot_inside, hot_chip)
    s_in[0, 0] = found[:, :HALF]
    s_in[0, 1] = found[:, HALF:]

    def send_z(h):
        for d in FAR_Z + [0]:
            for ds in range(SEG):
                if d or ds:
                    remote(s_in.at[h, lax.rem(seg + ds, SEG)], s_all.at[h, seg, y, x, z],
                           gone.at[4 + h], come.at[4 + h], zpeer(d, ds))
        local(s_in.at[h, seg], s_all.at[h, seg, y, x, z], come.at[4 + h])

    def sent_z(h):
        settled(b1.at[pl.ds(0, 3)], gone.at[4 + h])

    first_axis, second_axis = (xpeer, ypeer), (ypeer, xpeer)

    def block(h, p, d, e):
        if p == 0:
            return s_all.at[h, 0, lax.rem(y + e, NY), lax.rem(x + NX - d, NX)]
        return s_all.at[h, 1, lax.rem(y + NY - d, NY), lax.rem(x + e, NX)]

    def send_block(h, p, d, e, kind, device):
        one = block(h, p, d, e)
        early = (kind == 1 and d % 2 == 0) or (kind == 2 and d % 2 == 1)
        recv = pass_sem.at[1, h, p, d] if early else come.at[6 + h]
        return remote(one, one, gone.at[(8 if kind == 3 else 6) + h], recv, device)

    def phase_own(h):
        along = [None] * 4
        for d in (2, 1, 3):
            along[d] = [remote(block(h, p, 0, 0), block(h, p, 0, 0), gone.at[10 + h],
                               pass_sem.at[0, h, p, d], first_axis[p](d)) for p in range(2)]
        up = [None] * 4
        down = [None] * 4
        up[0] = [send_block(h, p, 0, 0, 1, second_axis[p](1)) for p in range(2)]
        down[0] = [send_block(h, p, 0, 0, 2, second_axis[p](3)) for p in range(2)]
        return along, up, down

    def phase_across(h, along, up, down):
        for d in (1, 3, 2):
            up[d], down[d] = [], []
            for p in range(2):
                along[d][p].wait_recv()
                up[d].append(send_block(h, p, d, 0, 1, second_axis[p](1)))
                down[d].append(send_block(h, p, d, 0, 2, second_axis[p](3)))

    def phase_relay(h, up, down):
        for d in (0, 1, 3, 2):
            for p in range(2):
                if d % 2 == 0:
                    up[d][p].wait_recv()
                    send_block(h, p, d, 3, 3, second_axis[p](1))
                else:
                    down[d][p].wait_recv()
                    send_block(h, p, d, 1, 3, second_axis[p](3))

    def phase_done(h):
        settled(s_all.at[h, 0], come.at[6 + h])

    def phase_sent(h):
        settled(s_all.at[h, 0], gone.at[6 + h])
        settled(s_all.at[h, 0, pl.ds(0, 2)], gone.at[8 + h])
        settled(s_all.at[h, :, pl.ds(0, 3), 0], gone.at[10 + h])

    def receivers(h, field):
        found = mm(field[:CHIPS], pick[0]) + mm(field[CHIPS:], pick[1])
        r_in[h] = found.reshape(NY, NX, NZ, 1, LANES)

    def r_send_y(h):
        for d in (2, 1, 3):
            remote(r_in.at[h, lax.rem(y + d, NY)], ry.at[h, y], gone.at[12 + h], come.at[8 + h], ypeer(d))
        local(r_in.at[h, y], ry.at[h, y], come.at[8 + h])

    def r_send_x(h):
        settled(ry.at[h], come.at[8 + h])
        for d in (2, 1, 3):
            remote(ry.at[h, :, lax.rem(x + d, NX)], rx.at[h, :, x], gone.at[14 + h], come.at[10 + h],
                   xpeer(d))
        local(ry.at[h, :, x], rx.at[h, :, x], come.at[10 + h])

    def r_send_z(h):
        settled(rx.at[h], come.at[10 + h])
        for d in FAR_Z + [0]:
            for ds in range(SEG):
                if d or ds:
                    remote(rx.at[h, :, :, lax.rem(z + d, NZ)], r_fin.at[h, seg, :, :, z],
                           gone.at[16 + h], come.at[12 + h], zpeer(d, ds))
        local(rx.at[h, :, :, z], r_fin.at[h, seg, :, :, z], come.at[12 + h])

    def r_sent(h):
        settled(r_in.at[h, pl.ds(0, 3)], gone.at[12 + h])
        settled(ry.at[h, :, pl.ds(0, 3)], gone.at[14 + h])

    def receivers_across(h):
        for g in range(SEG):
            rt[g] = mm_nt(small, r_fin[h, g].reshape(CHIPS, LANES).astype(BF))

    small = eye[:LANES, :LANES]
    send_z(0)
    receivers(0, field)
    r_send_y(0)
    settled(x1, come.at[3])
    field = filter_half(1, x1[...].reshape(CHIPS, 2 * WIDE), chan, limit_ref, tables, twist)
    found = source_rows(field, hot_inside, hot_chip)
    s_in[1, 0] = found[:, :HALF]
    s_in[1, 1] = found[:, HALF:]
    send_z(1)
    receivers(1, field)
    r_send_y(1)
    r_send_x(0)
    settled(s_all.at[0, 0, 0, pl.ds(0, 2)], come.at[4])
    along0, up0, down0 = phase_own(0)
    settled(a.at[0, pl.ds(0, NZ - 1)], gone.at[0])
    settled(b1.at[pl.ds(0, PLANE - 1)], gone.at[1])
    settled(b0.at[pl.ds(0, PLANE - 1)], gone.at[2])
    settled(b2.at[pl.ds(0, NZ - 1)], gone.at[3])
    r_send_x(1)
    r_send_z(0)
    phase_across(0, along0, up0, down0)
    settled(s_all.at[1, 0, 0, pl.ds(0, 2)], come.at[5])
    along1, up1, down1 = phase_own(1)
    r_send_z(1)
    phase_relay(0, up0, down0)
    sent_z(0)
    sent_z(1)
    r_sent(0)
    r_sent(1)
    phase_across(1, along1, up1, down1)
    phase_done(0)
    sources_across(0, s_all, flat, st, small)
    phase_relay(1, up1, down1)
    settled(r_fin.at[0], come.at[12])
    receivers_across(0)
    lag_load.wait()
    correlate_half(0, st, rt, lag, cross, total, None)
    settled(b1.at[pl.ds(0, 12)], gone.at[16])
    settled(b1.at[pl.ds(0, 12)], gone.at[17])
    phase_sent(0)
    settled(r_fin.at[1], come.at[13])
    receivers_across(1)
    phase_done(1)
    sources_across(1, s_all, flat, st, small)

    def keep(b, result):
        part = slice(b * VBLOCK, (b + 1) * VBLOCK)
        result_buf[part] = result.astype(BF).reshape(VBLOCK, RECS, LAGS)
        at = pl.ds(b * VBLOCK, VBLOCK)
        local(result_buf.at[at], out_ref.at[at], late_sem.at[6])

    correlate_half(1, st, rt, lag, cross, total, keep)
    phase_sent(1)
    settled(result_buf, late_sem.at[6])


def correlations(records, limits, sources):
    tables, twist, pick = filter_tables()
    hbm = pl.BlockSpec(memory_space=pl.ANY)
    dma = pltpu.SemaphoreType.DMA
    by_z = pltpu.VMEM((NZ, PLANE, 2 * WIDE), BF)
    by_plane = pltpu.VMEM((PLANE, NZ, 2 * WIDE), BF)
    grid_of = pltpu.VMEM((2, NY, NX, NZ, 1, LANES), F32)
    return pl.pallas_call(
        whole_kernel,
        out_shape=jax.ShapeDtypeStruct((HALF, RECS, LAGS), BF),
        in_specs=[hbm] * 8,
        out_specs=hbm,
        scratch_shapes=[
            pltpu.VMEM((2, SEG, NY, NX, NZ, SEQS, HALF), BF),
            pltpu.VMEM((2, SEG, NY, NX, NZ, 1, LANES), F32),
            pltpu.VMEM((CHIPS * SEQS, HALF), F32),
            pltpu.VMEM((SEG, SEQS, HALF, CHIPS), F32),
            pltpu.VMEM((SEG, LANES, CHIPS), F32),
            pltpu.VMEM((HALF // VBLOCK, VBLOCK * RECS, NF), BF),
            pltpu.VMEM((HALF // VBLOCK, VBLOCK * RECS, LAGS), F32),
            pltpu.VMEM((2, NF, LAGS), BF),
            pltpu.SMEM((1, NF), jnp.int32),
            pltpu.VMEM((1, NVS), jnp.int32),
            pltpu.VMEM((HALF, RECS, LAGS), BF),
            pltpu.VMEM((RADIX, M_DEV, CH_DEV, QUARTER), BF),
            pltpu.VMEM((STEPS, RADIX, KBLOCK, 2 * CHIPS), BF),
            pltpu.VMEM((6, ROWS, 2 * CHIPS), F32),
            pltpu.VMEM(tables.shape, BF),
            pltpu.VMEM(twist.shape, F32),
            pltpu.VMEM(pick.shape, BF),
            pltpu.VMEM((2, NZ, PLANE, 2 * WIDE), BF),
            by_z, by_plane, by_plane, by_plane, by_plane, by_z, by_z,
            pltpu.VMEM((2, SEG, SEQS, HALF), BF),
            grid_of, grid_of, grid_of,
            dma((2, STEPS)), dma((7,)), dma((14,)), dma((18,)), dma((2, 2, 2, NX)),
        ],
        compiler_params=pltpu.CompilerParams(
            collective_id=0, has_side_effects=True, vmem_limit_bytes=57 << 20
        ),
        cost_estimate=pl.CostEstimate(flops=6 << 30, bytes_accessed=12 << 20, transcendentals=0),
        name="correlations",
    )(
        records,
        jnp.asarray(time_tables()),
        limits.reshape(1, NF),
        sources.reshape(1, NVS),
        jnp.asarray(tables),
        jnp.asarray(twist),
        jnp.asarray(pick),
        jnp.asarray(lag_table()),
    )

def settle_kernel(from_ref, to_ref, held, sems):
    count = 2
    parts = [pl.ds(k * (HALF // count), HALF // count) for k in range(count)]
    into = [pltpu.make_async_copy(from_ref.at[p], held.at[p], sems.at[0, k])
            for k, p in enumerate(parts)]
    onto = [pltpu.make_async_copy(held.at[p], to_ref.at[p], sems.at[1, k])
            for k, p in enumerate(parts)]
    for copy in into:
        copy.start()
    for one, two in zip(into, onto):
        one.wait()
        two.start()
    for copy in onto:
        copy.wait()


def shards(records, limits, sources):
    result = correlations(records, limits, sources)
    hbm = pl.BlockSpec(memory_space=pl.ANY)
    return pl.pallas_call(
        settle_kernel,
        out_shape=jax.ShapeDtypeStruct(result.shape, result.dtype),
        in_specs=[hbm],
        out_specs=hbm,
        scratch_shapes=[
            pltpu.VMEM(result.shape, result.dtype), pltpu.SemaphoreType.DMA((2, 2))
        ],
        compiler_params=pltpu.CompilerParams(vmem_limit_bytes=57 << 20),
        name="settle",
    )(result)


def solution(mesh):
    in_specs = (P(None, "chan", None), P(), P())
    out_specs = P("segment", "chan", None)
    return jax.shard_map(shards, mesh=mesh, in_specs=in_specs, out_specs=out_specs, check_vma=False)
```
